32 devices in a mesh: dp: 8 (over z, x), ctx: 4 (over y, core).
Axes of the slice: x: 2, y: 2, z: 4, core: 2. Of those that a mesh axis runs over, the one named last changes fastest.
Arguments:
- scan_input: bfloat16 [8, 512, 4096], P('dp', 'ctx'), may hold values from -6 to 6
- step_raw: bfloat16 [8, 512, 4096], P('dp', 'ctx'), may hold values from -3 to 11
- input_proj: float32 [8, 16, 512], P('dp', None, 'ctx'), may hold values from -6 to 6
- output_proj: float32 [8, 16, 512], P('dp', None, 'ctx'), may hold values from -6 to 6
- out_cotangent: bfloat16 [8, 512, 4096], P('dp', 'ctx'), may hold values from -6 to 6
- conv_weight: float32 [4, 4096], replicated, may hold values from -3 to 3
- conv_bias: float32 [4096], replicated, may hold values from -0.5 to 0.5
- step_bias: float32 [4096], replicated, may hold values from -9 to -1
- decay_log: float32 [16, 4096], replicated, may hold values from -2.5 to 2.8
- skip_weight: float32 [4096], replicated, may hold values from 0.5 to 1.5
Outputs:
- grad_input: bfloat16 [8, 512, 4096], P('dp', 'ctx')
- grad_input_proj: float32 [8, 16, 512], P('dp', None, 'ctx')
- grad_output_proj: float32 [8, 16, 512], P('dp', None, 'ctx')
- convolution_weight_gradient: float32 [4, 4096], replicated
- grad_conv_bias: float32 [4096], replicated
- step_bias_gradient: float32 [4096], replicated
- grad_decay_log: float32 [16, 4096], replicated
- grad_skip_weight: float32 [4096], replicated
The draws below stay inside these ranges and needn't reach their ends.
All inputs are finite; a program needn't handle non-finite values.
Results may differ from the reference program's by a relative error of at most 0.009.
Values may be sent and summed in bfloat16 or wider, within the bound.
No kernel may reach another device: no remote copies, remote signals or barrier semaphores. Data moves between devices by JAX's collectives and lax.ppermute only.
A program may use at most 128 MiB of HBM per device.

```python
from functools import partial
import jax
import jax.numpy as jnp
from jax import lax

CH = 4096
NST = 16
KCONV = 4
DOCUMENT_LENGTH = 512
DOCUMENT_COUNT = 8


def draw_step_raw(key, part):
    first_key, random_key_second, third_key = jax.random.split(key, 3)
    reference_output = jnp.clip(0.5 * jax.random.normal(first_key, (DOCUMENT_COUNT, DOCUMENT_LENGTH, CH), jnp.float32), -3.0, 3.0)
    piece_groups = jax.random.bernoulli(random_key_second, 4.0 / DOCUMENT_LENGTH, (DOCUMENT_COUNT, DOCUMENT_LENGTH, 1)).astype(jnp.float32)
    state_height = jax.random.uniform(third_key, (DOCUMENT_COUNT, DOCUMENT_LENGTH, 1), jnp.float32, 5.0, 8.0)
    return jnp.clip(reference_output + piece_groups * state_height, -3.0, 11.0).astype(jnp.bfloat16)


def block_scale(rng, dims, pieces, low, top_value):
    level, own = 1.0, jax.random.fold_in(rng, 6)
    for dim, blocks in pieces:
        steps = jnp.exp(jax.random.uniform(jax.random.fold_in(own, dim), (blocks,), jnp.float32, low / len(pieces), top_value / len(pieces)))
        level = level * jnp.repeat(steps, dims[dim] // blocks).reshape([-1 if axis == dim else 1 for axis in range(len(dims))])
    return level


def bell_draw(rng, extent, spread, limit, pieces=(), dtype=jnp.bfloat16):
    values = spread * jax.random.normal(rng, extent, jnp.float32)
    if pieces:
        values = values * block_scale(rng, extent, pieces, -0.22, 0.18)
    return jnp.clip(values, -limit, limit).astype(dtype)


def setup_inputs(seed: int = 0) -> dict:
    key_list = jax.random.split(jax.random.key(seed), 11)
    return {
        "scan_input": bell_draw(key_list[0], (DOCUMENT_COUNT, DOCUMENT_LENGTH, CH), 1.0, 6.0, ((0, 8), (1, 4))),
        "step_raw": draw_step_raw(jax.random.fold_in(key_list[10], 71), 0),
        "input_proj": bell_draw(key_list[2], (DOCUMENT_COUNT, NST, DOCUMENT_LENGTH), 1.0, 6.0, ((0, 8), (2, 4)), jnp.float32),
        "output_proj": bell_draw(key_list[3], (DOCUMENT_COUNT, NST, DOCUMENT_LENGTH), 1.0, 6.0, ((0, 8), (2, 4)), jnp.float32),
        "out_cotangent": bell_draw(key_list[4], (DOCUMENT_COUNT, DOCUMENT_LENGTH, CH), 1.0, 6.0, ((0, 8), (1, 4))),
        "conv_weight": bell_draw(key_list[5], (KCONV, CH), KCONV ** -0.5, 3.0, (), jnp.float32),
        "conv_bias": jnp.clip(jax.random.uniform(key_list[6], (CH,), jnp.float32, -0.5, 0.5), -0.5, 0.5),
        "step_bias": jnp.clip(jax.random.uniform(key_list[7], (CH,), jnp.float32, -9.0, -1.0), -9.0, -1.0),
        "decay_log": jnp.clip(jax.random.uniform(key_list[8], (NST, CH), jnp.float32, -2.5, 2.8), -2.5, 2.8),
        "skip_weight": jnp.clip(jax.random.uniform(key_list[9], (CH,), jnp.float32, 0.5, 1.5), 0.5, 1.5),
    }


def advance(carry_state, inputs, decay_rate):
    step_now, activation, b_col, c_col = inputs
    carry_state = jnp.exp(step_now[None, :] * decay_rate) * carry_state + b_col[:, None] * (step_now * activation)[None, :]
    return (carry_state, lax.optimization_barrier(jnp.sum(c_col[:, None] * carry_state, axis=0)))

def convolve(extended, conv_weight, conv_bias, length):
    running = conv_bias + conv_weight[0] * extended[0:length]
    for offset in range(1, conv_weight.shape[0]):
        running = running + conv_weight[offset] * extended[offset:offset + length]
    return jax.nn.silu(running)

def forward_document(input_float, b_matrix, c_matrix, conv_weight, conv_bias, step_bias, decay_log, skip_weight, step_float):
    length = input_float.shape[0]
    padding = jnp.zeros((conv_weight.shape[0] - 1, input_float.shape[1]), jnp.float32)
    extended = jnp.concatenate([padding, input_float], axis=0)
    activation = convolve(extended, conv_weight, conv_bias, length)
    step_size = jax.nn.softplus(step_float + step_bias)
    decay_rate = -jnp.exp(decay_log)
    start_state = jnp.zeros((decay_log.shape[0], input_float.shape[1]), jnp.float32)
    _, scanned = lax.scan(partial(advance, decay_rate=decay_rate), start_state, (step_size, activation, b_matrix.T, c_matrix.T))
    return scanned + skip_weight * activation

def reference(scan_input, step_raw, input_proj, output_proj, out_cotangent, conv_weight, conv_bias, step_bias, decay_log, skip_weight):

    def one_document(doc_items):
        input_doc, step_doc, b_doc, c_doc, grad_doc = doc_items
        step_float = step_doc.astype(jnp.float32)

        def forward(input_float, b_matrix, c_matrix, weight_taps, bias_taps, bias_steps, log_rates, direct_weight):
            return forward_document(input_float, b_matrix, c_matrix, weight_taps, bias_taps, bias_steps, log_rates, direct_weight, step_float)
        _, pullback = jax.vjp(forward, input_doc.astype(jnp.float32), b_doc, c_doc, conv_weight, conv_bias, step_bias, decay_log, skip_weight)
        return pullback(grad_doc.astype(jnp.float32))
    gradients = lax.map(one_document, (scan_input, step_raw, input_proj, output_proj, out_cotangent))
    return (gradients[0].astype(jnp.bfloat16), gradients[1], gradients[2], lax.optimization_barrier(jnp.sum(gradients[3], axis=0)), lax.optimization_barrier(jnp.sum(gradients[4], axis=0)), lax.optimization_barrier(jnp.sum(gradients[5], axis=0)), lax.optimization_barrier(jnp.sum(gradients[6], axis=0)), lax.optimization_barrier(jnp.sum(gradients[7], axis=0)))
```

```python
import math

import jax
import jax.numpy as jnp
from jax import lax
from jax.experimental import pallas as pl
from jax.experimental.pallas import tpu as pltpu
from jax.sharding import PartitionSpec as P

F32 = jnp.float32
BF16 = jnp.bfloat16
LOG2E = 1.0 / math.log(2.0)
BLOCK = 16
LANES = 128
WIDTH = 512
VMEM = 60 * 1024 * 1024


def lane_slices(width):
    return [slice(j, j + LANES) for j in range(0, width, LANES)]


def row_of(ref, t, j):
    row = ref[j, pl.ds(t, 8, stride=0), :]
    return jnp.concatenate([row, row], axis=0)


def put(ref, rows, value):
    for j in range(ref.shape[0]):
        ref[j, rows, :] = value[:, j * LANES : (j + 1) * LANES]


def take(ref, rows):
    return jnp.concatenate([ref[j, rows, :] for j in range(ref.shape[0])], axis=1)


def joined_tiles(ref):
    return jnp.concatenate([ref[j] for j in range(ref.shape[0])], axis=1)


def row_sum(value):
    total = value[0:8]
    for r in range(8, value.shape[0], 8):
        total = total + value[r : r + 8]
    return total


def set_rates(dl_ref, rates):
    for j, s in enumerate(lane_slices(dl_ref.shape[1])):
        rates[j] = -jnp.exp(dl_ref[:, s]) * LOG2E


def ends_kernel(x_ref, rim_ref, step_ref, dy_ref, bb_ref, cm_ref, cw_ref, cb_ref, sb_ref, dl_ref,
                out_ref, dls, dus, dyf, u_ref, sig_ref, slope_ref, dub_ref, xe, xs, rates):
    length, width = x_ref.shape
    states = dl_ref.shape[0]
    taps = cw_ref.shape[0]
    blocks = length // BLOCK
    weights = [cw_ref[k : k + 1, :] for k in range(taps)]
    bias, shift = cb_ref[...], sb_ref[...]
    slices = lane_slices(width)
    set_rates(dl_ref, rates)
    xe[0:8, :] = jnp.zeros((8, width), F32)
    xe[8 - (taps - 1) : 8, :] = rim_ref[...].astype(F32)
    total = jnp.zeros((8, width), F32)
    for b in range(blocks):
        rows = slice(b * BLOCK, (b + 1) * BLOCK)
        xe[8 + b * BLOCK : 8 + (b + 1) * BLOCK, :] = x_ref[rows, :].astype(F32)
        put(dyf, rows, dy_ref[rows, :].astype(F32))
        z = jnp.exp(step_ref[rows, :].astype(F32) + shift)
        series = z * (1.0 - z * (0.5 - z * (1.0 / 3.0 - 0.25 * z)))
        delta = jnp.where(z < 0.015625, series, jnp.log(1.0 + z))
        p = bias
        for k in range(taps):
            first = b * BLOCK + 9 - taps + k
            p = p + weights[k] * xe[first : first + BLOCK, :]
        gate = 1.0 / (1.0 + jnp.exp(-p))
        u = p * gate
        du = delta * u
        put(dls, rows, delta)
        put(dus, rows, du)
        u_ref[rows, :] = u
        sig_ref[rows, :] = z / (1.0 + z)
        slope_ref[rows, :] = gate + u * (1.0 - gate)
        dub_ref[rows, :] = du.astype(BF16)
        total = total + row_sum(delta)
    total = jnp.sum(total, axis=0, keepdims=True)

    def block(b, carry):
        state, decay, adjoint = carry
        state, decay = list(state), list(decay)
        base = pl.multiple_of(b * BLOCK, BLOCK)
        for i in range(BLOCK):
            t = base + i
            column = bb_ref[pl.ds(pl.multiple_of(t * states, states), states), :]
            for j in range(len(slices)):
                a = jnp.exp2(row_of(dls, t, j) * rates[j])
                state[j] = a * state[j] + column * row_of(dus, t, j)
                decay[j] = decay[j] * a
                xs[j, i * states : (i + 1) * states, :] = (decay[j] * row_of(dyf, t, j)).astype(BF16)
        adjoint = adjoint + jnp.dot(
            cm_ref[pl.ds(pl.multiple_of(b * states, states), states), :], joined_tiles(xs),
            preferred_element_type=F32)
        return tuple(state), tuple(decay), adjoint

    zero = tuple(jnp.zeros((states, LANES), F32) for _ in slices)
    one = tuple(jnp.ones((states, LANES), F32) for _ in slices)
    state, _, adjoint = lax.fori_loop(0, blocks, block, (zero, one, jnp.zeros((states, width), F32)))
    for j, s in enumerate(slices):
        out_ref[0:states, s] = state[j].astype(BF16)
    out_ref[states : 2 * states, :] = adjoint.astype(BF16)
    high = total.astype(BF16)
    rest = total - high.astype(F32)
    middle = rest.astype(BF16)
    low = (rest - middle.astype(F32)).astype(BF16)
    row = lax.broadcasted_iota(jnp.int32, (16, width), 0)
    packed = jnp.where(row == 0, high.astype(F32), jnp.where(row == 1, middle.astype(F32), low.astype(F32)))
    out_ref[2 * states : 2 * states + 16, :] = packed.astype(BF16)


def main_kernel(si_ref, ai_ref, x_ref, rim_ref, dy_ref, dls, dus, dyf, u_ref, sig_ref, slope_ref, dub_ref,
                bb_ref, cb2_ref, bd_ref, cw_ref, dl_ref, sk_ref,
                gin_ref, borrow_ref, tail_ref, gb_ref, gc_ref, pg_ref,
                xe, ahs, hb, dpe, acc, rates, naturals):
    length, width = x_ref.shape
    states = dl_ref.shape[0]
    taps = cw_ref.shape[0]
    blocks = length // BLOCK
    slices = lane_slices(width)
    pairs = [slices[j : j + 2] for j in range(0, len(slices), 2)]

    @pl.when(pl.program_id(0) == 0)
    def _():
        gb_ref[...] = jnp.zeros_like(gb_ref)
        gc_ref[...] = jnp.zeros_like(gc_ref)

    set_rates(dl_ref, rates)
    for j, s in enumerate(slices):
        naturals[j] = (-jnp.exp(dl_ref[:, s])).astype(BF16)
    lane = lax.broadcasted_iota(jnp.int32, (states, length), 1)

    def forward(b, carry):
        state, gc = carry
        state = list(state)
        base = pl.multiple_of(b * BLOCK, BLOCK)
        for i in range(BLOCK):
            t = base + i
            rows = pl.ds(pl.multiple_of(t * states, states), states)
            column = bb_ref[rows, :]
            for j in range(len(slices)):
                a = jnp.exp2(row_of(dls, t, j) * rates[j])
                kept = a * state[j]
                ahs[j, rows, :] = kept.astype(BF16)
                state[j] = kept + column * row_of(dus, t, j)
                hb[j, i * states : (i + 1) * states, :] = state[j].astype(BF16)
        product = lax.dot_general(joined_tiles(hb), dy_ref[...], (((1,), (1,)), ((), ())),
                                  preferred_element_type=F32)
        for i in range(BLOCK):
            gc = jnp.where(lane == base + i, product[i * states : (i + 1) * states], gc)
        return tuple(state), gc

    nothing = jnp.zeros((states, length), F32)
    _, gc = lax.fori_loop(0, blocks, forward, (tuple(si_ref[:, s] for s in slices), nothing))
    gc_ref[...] += gc

    acc[...] = jnp.zeros_like(acc)
    dpe[0:8, :] = jnp.zeros((8, width), F32)
    dpe[length + 8 : length + 16, :] = jnp.zeros((8, width), F32)
    rows_of = lax.broadcasted_iota(jnp.int32, (BLOCK, BLOCK * states), 0)
    cols_of = lax.broadcasted_iota(jnp.int32, (BLOCK, BLOCK * states), 1)
    over_states = jnp.where(rows_of == cols_of // states, 1.0, 0.0).astype(BF16)
    rows_of = lax.broadcasted_iota(jnp.int32, (states, BLOCK * states), 0)
    cols_of = lax.broadcasted_iota(jnp.int32, (states, BLOCK * states), 1)
    over_steps = jnp.where(rows_of == cols_of % states, 1.0, 0.0).astype(BF16)

    def backward(n, carry):
        adjoint, gb, rates_sum = carry
        adjoint, rates_sum = list(adjoint), list(rates_sum)
        b = blocks - 1 - n
        base = pl.multiple_of(b * BLOCK, BLOCK)
        kept = {}
        for i in reversed(range(BLOCK)):
            t = base + i
            rows = pl.ds(pl.multiple_of(t * states, states), states)
            column = cb2_ref[rows, :]
            for j in range(len(slices)):
                delta = row_of(dls, t, j)
                g = column * row_of(dyf, t, j) + adjoint[j]
                adjoint[j] = jnp.exp2(delta * rates[j]) * g
                low = g.astype(BF16)
                q = low * ahs[j, rows, :]
                kept[i, j] = low, q * naturals[j], q * delta.astype(BF16)

        def operand(pair, which):
            return jnp.concatenate(
                [jnp.concatenate([kept[i, j][which] for i in range(BLOCK)], axis=0) for j in pair], axis=1)

        ddu, dwn, product = [], [], None
        for m in range(len(pairs)):
            pair = (2 * m, 2 * m + 1)
            g_block = operand(pair, 0)
            ddu.append(jnp.dot(bd_ref[pl.ds(base, BLOCK), :], g_block, preferred_element_type=F32))
            dwn.append(jnp.dot(over_states, operand(pair, 1), preferred_element_type=F32))
            rates_sum[m] = rates_sum[m] + jnp.dot(over_steps, operand(pair, 2), preferred_element_type=F32)
            part = lax.dot_general(g_block, dub_ref[:, 2 * m * LANES : 2 * (m + 1) * LANES],
                                   (((1,), (1,)), ((), ())), preferred_element_type=F32)
            product = part if product is None else product + part
        for i in range(BLOCK):
            gb = jnp.where(lane == base + i, product[i * states : (i + 1) * states], gb)
        rows = pl.ds(base, BLOCK)
        ddu, dwn = jnp.concatenate(ddu, axis=1), jnp.concatenate(dwn, axis=1)
        dy, u = take(dyf, rows), u_ref[rows, :]
        grad_v = (ddu * u + dwn) * sig_ref[rows, :]
        grad_p = (ddu * take(dls, rows) + sk_ref[...] * dy) * slope_ref[rows, :]
        dpe[pl.ds(pl.multiple_of(base + 8, 8), BLOCK), :] = grad_p
        acc[taps] += row_sum(grad_p)
        acc[taps + 1] += row_sum(grad_v)
        acc[taps + 2] += row_sum(dy * u)
        return tuple(adjoint), gb, tuple(rates_sum)

    start = (tuple(ai_ref[:, s] for s in slices), nothing,
             tuple(jnp.zeros((states, 2 * LANES), F32) for _ in pairs))
    _, gb, rates_sum = lax.fori_loop(0, blocks, backward, start)
    gb_ref[...] += gb
    rates_sum = jnp.concatenate(rates_sum, axis=1)
    for j, s in enumerate(slices):
        pg_ref[0:states, s] = rates_sum[:, s] * (-jnp.exp(dl_ref[:, s]))

    weights = [cw_ref[k : k + 1, :] for k in range(taps)]
    xe[0:8, :] = jnp.zeros((8, width), F32)
    xe[8 - (taps - 1) : 8, :] = rim_ref[...].astype(F32)
    sums = [jnp.zeros((8, width), F32) for _ in range(taps)]
    for b in range(blocks):
        rows = slice(b * BLOCK, (b + 1) * BLOCK)
        xe[8 + b * BLOCK : 8 + (b + 1) * BLOCK, :] = x_ref[rows, :].astype(F32)
        grad_p = dpe[8 + b * BLOCK : 8 + (b + 1) * BLOCK, :]
        grad_x = weights[taps - 1] * grad_p
        for k in range(taps):
            first = b * BLOCK + 9 - taps + k
            sums[k] = sums[k] + row_sum(grad_p * xe[first : first + BLOCK, :])
            if k < taps - 1:
                first = b * BLOCK + 7 + taps - k
                grad_x = grad_x + weights[k] * dpe[first : first + BLOCK, :]
        gin_ref[rows, :] = grad_x.astype(BF16)
        if b == blocks - 1:
            tail_ref[...] = grad_x
    grad_rim = weights[0] * dpe[taps - 1 : taps + 7, :]
    for k in range(1, taps):
        grad_rim = grad_rim + weights[k] * dpe[taps - 1 - k : taps + 7 - k, :]
    borrow_ref[...] = grad_rim[8 - borrow_ref.shape[0] : 8].astype(BF16)
    small = [jnp.sum(a, axis=0, keepdims=True) for a in sums]
    small += [jnp.sum(acc[taps + k], axis=0, keepdims=True) for k in range(3)]
    row = lax.broadcasted_iota(jnp.int32, (8, width), 0)
    packed = jnp.zeros((8, width), F32)
    for k in range(taps + 3):
        packed = jnp.where(row == k, small[k], packed)
    pg_ref[states : states + 8, :] = packed


def flipped(value, axis, bit):
    return lax.ppermute(value, axis, [(k, k ^ bit) for k in range(lax.axis_size(axis))])


def add_up(value):
    inner, outer = lax.axis_size("ctx"), lax.axis_size("dp")
    if inner & (inner - 1) or outer & (outer - 1):
        return lax.psum(value, ("dp", "ctx"))
    me = lax.axis_index("ctx")
    bits = [1 << k for k in range(inner.bit_length() - 1)]
    for bit in bits:
        half = value.shape[1] // 2
        upper = (me // bit) % 2
        give = lax.dynamic_slice_in_dim(value, (1 - upper) * half, half, 1)
        got = flipped(give, "ctx", bit)
        value = lax.dynamic_slice_in_dim(value, upper * half, half, 1) + got
    for k in range(outer.bit_length() - 1):
        value = value + flipped(value, "dp", 1 << k)
    for bit in reversed(bits):
        got = flipped(value, "ctx", bit)
        upper = (me // bit) % 2 == 1
        value = jnp.concatenate([jnp.where(upper, got, value), jnp.where(upper, value, got)], axis=1)
    return value


def entering(ends, decay_log):
    states = decay_log.shape[0]
    count, place = lax.axis_size("ctx"), lax.axis_index("ctx")
    rate = -jnp.exp(decay_log)

    def opened(piece):
        total = jnp.sum(piece[2 * states : 2 * states + 3].astype(F32), axis=0, keepdims=True)
        return piece[:states].astype(F32), piece[states : 2 * states].astype(F32), jnp.exp(rate * total)

    if count == 4:
        upper, late = place % 2 == 1, place // 2 == 1
        mine, other = opened(ends), opened(flipped(ends, "ctx", 1))
        pick = lambda a, b: jnp.where(upper, a, b)
        first, second = [pick(b, a) for a, b in zip(mine, other)], [pick(a, b) for a, b in zip(mine, other)]
        both = jnp.where(late, second[1] * first[2] + first[1], first[0] * second[2] + second[0])
        got = flipped(both.astype(BF16), "ctx", 2).astype(F32)
        before, after = jnp.where(late, got, 0.0), jnp.where(late, 0.0, got)
        state = jnp.where(upper, before * first[2] + first[0], before)
        adjoint = jnp.where(upper, after, after * second[2] + second[1])
        return state, adjoint
    gathered = lax.all_gather(ends, "ctx")
    state = adjoint = jnp.zeros(decay_log.shape, F32)
    for k in range(count - 1):
        end, _, decay = opened(gathered[k])
        state = jnp.where(k < place, decay * state + end, state)
    for k in range(count - 1, 0, -1):
        _, end, decay = opened(gathered[k])
        adjoint = jnp.where(k > place, decay * adjoint + end, adjoint)
    return state, adjoint


def per_device(scan_input, step_raw, input_proj, output_proj, out_cotangent, conv_weight, conv_bias, step_bias,
               decay_log, skip_weight):
    documents, length, channels = scan_input.shape
    states, taps = decay_log.shape[0], conv_weight.shape[0]
    rim = taps - 1
    blocks = length // BLOCK
    count = lax.axis_size("ctx")
    forth = [(k, k + 1) for k in range(count - 1)]
    back = [(k + 1, k) for k in range(count - 1)]
    flat = lambda a: a.reshape(1, channels)
    tiles = WIDTH // LANES
    work = length * states * channels

    def whole(a):
        return pl.BlockSpec(a.shape, lambda i: (0,) * a.ndim)

    def chunk(rows):
        return pl.BlockSpec((rows, WIDTH), lambda i: (0, i))

    tiled = pl.BlockSpec((tiles, length, LANES), lambda i: (i, 0, 0))
    summed = pl.BlockSpec((states, length), lambda i: (0, 0))
    params = pltpu.CompilerParams(vmem_limit_bytes=VMEM, dimension_semantics=("arbitrary",))
    shape = jax.ShapeDtypeStruct

    def one(x, step, b_proj, c_proj, dy):
        rims = lax.ppermute(x[length - rim :, :], "ctx", forth)
        b_rows, c_rows = b_proj.T, c_proj.T
        b_wide = jnp.broadcast_to(b_rows.reshape(length * states, 1), (length * states, LANES))
        c_wide = jnp.broadcast_to(c_rows.reshape(length * states, 1), (length * states, LANES))
        steps_eye, states_eye = jnp.eye(BLOCK, dtype=F32), jnp.eye(states, dtype=F32)
        b_diag = (b_rows.reshape(blocks, 1, BLOCK, states) * steps_eye[None, :, :, None]).reshape(
            length, BLOCK * states).astype(BF16)
        c_diag = (c_rows.reshape(blocks, 1, BLOCK, states) * states_eye[None, :, None, :]).reshape(
            blocks * states, BLOCK * states).astype(BF16)
        long = shape((channels // LANES, length, LANES), F32)
        plain = shape((length, channels), F32)
        ends, *saved = pl.pallas_call(
            ends_kernel,
            grid=(channels // WIDTH,),
            in_specs=[chunk(length), chunk(rim), chunk(length), chunk(length), whole(b_wide), whole(c_diag),
                      chunk(taps), chunk(1), chunk(1), chunk(states)],
            out_specs=[chunk(2 * states + 16)] + [tiled] * 3 + [chunk(length)] * 4,
            out_shape=[shape((2 * states + 16, channels), BF16), long, long, long, plain, plain, plain,
                       shape((length, channels), BF16)],
            scratch_shapes=[pltpu.VMEM((length + 16, WIDTH), F32),
                            pltpu.VMEM((tiles, BLOCK * states, LANES), BF16),
                            pltpu.VMEM((tiles, states, LANES), F32)],
            compiler_params=params,
            cost_estimate=pl.CostEstimate(flops=8 * work, bytes_accessed=20 * length * channels, transcendentals=work),
        )(x, rims, step, dy, b_wide, c_diag, conv_weight, flat(conv_bias), flat(step_bias), decay_log)
        state_in, adjoint_in = entering(ends, decay_log)
        return pl.pallas_call(
            main_kernel,
            grid=(channels // WIDTH,),
            in_specs=[chunk(states), chunk(states), chunk(length), chunk(rim), chunk(length)] + [tiled] * 3
            + [chunk(length)] * 4 + [whole(b_wide), whole(c_wide), whole(b_diag), chunk(taps), chunk(states), chunk(1)],
            out_specs=[chunk(length), chunk(rim), chunk(BLOCK), summed, summed, chunk(states + 8)],
            out_shape=[shape((length, channels), BF16), shape((rim, channels), BF16), shape((BLOCK, channels), F32),
                       shape((states, length), F32), shape((states, length), F32),
                       shape((states + 8, channels), F32)],
            scratch_shapes=[pltpu.VMEM((length + 16, WIDTH), F32),
                            pltpu.VMEM((tiles, length * states, LANES), BF16),
                            pltpu.VMEM((tiles, BLOCK * states, LANES), BF16),
                            pltpu.VMEM((length + 16, WIDTH), F32),
                            pltpu.VMEM((taps + 3, 8, WIDTH), F32),
                            pltpu.VMEM((tiles, states, LANES), F32),
                            pltpu.VMEM((tiles, states, LANES), BF16)],
            compiler_params=params,
            cost_estimate=pl.CostEstimate(flops=20 * work, bytes_accessed=24 * length * channels, transcendentals=2 * work),
        )(state_in, adjoint_in, x, rims, dy, *saved, b_wide, c_wide, b_diag, conv_weight, decay_log,
          flat(skip_weight))

    outs = []
    for d in range(documents):
        gin, borrow, tail, gb, gc, sums = one(
            scan_input[d], step_raw[d], input_proj[d], output_proj[d], out_cotangent[d])
        given = lax.ppermute(borrow, "ctx", back).astype(F32)
        tail = (tail + jnp.pad(given, ((BLOCK - rim, 0), (0, 0)))).astype(BF16)
        gin = lax.dynamic_update_slice(gin, tail, (length - BLOCK, 0))
        outs.append((gin, gb, gc, sums))
    sums = add_up(sum(o[3] for o in outs))
    return (
        jnp.stack([o[0] for o in outs]),
        jnp.stack([o[1] for o in outs]),
        jnp.stack([o[2] for o in outs]),
        sums[states : states + taps],
        sums[states + taps],
        sums[states + taps + 1],
        sums[:states],
        sums[states + taps + 2],
    )


def solution(mesh):
    split, columns = P("dp", "ctx", None), P("dp", None, "ctx")
    return jax.shard_map(
        per_device,
        mesh=mesh,
        in_specs=(split, split, columns, columns, split, P(), P(), P(), P(), P()),
        out_specs=(split, columns, columns, P(), P(), P(), P(), P()),
        check_vma=False,
    )
```

```python
import math

import jax
import jax.numpy as jnp
from jax import lax
from jax.experimental import pallas as pl
from jax.experimental.pallas import tpu as pltpu
from jax.sharding import PartitionSpec as P

F32 = jnp.float32
BF16 = jnp.bfloat16
LOG2E = 1.0 / math.log(2.0)
BLOCK = 16
LANES = 128
WIDTH = 512
VMEM = 60 * 1024 * 1024


def lane_slices(width):
    return [slice(j, j + LANES) for j in range(0, width, LANES)]


def row_of(ref, t, j):
    row = ref[j, pl.ds(t, 8, stride=0), :]
    return jnp.concatenate([row, row], axis=0)


def put(ref, rows, value):
    for j in range(ref.shape[0]):
        ref[j, rows, :] = value[:, j * LANES : (j + 1) * LANES]


def take(ref, rows):
    return jnp.concatenate([ref[j, rows, :] for j in range(ref.shape[0])], axis=1)


def joined_tiles(ref):
    return jnp.concatenate([ref[j] for j in range(ref.shape[0])], axis=1)


def row_sum(value):
    total = value[0:8]
    for r in range(8, value.shape[0], 8):
        total = total + value[r : r + 8]
    return total


def set_rates(dl_ref, rates):
    for j, s in enumerate(lane_slices(dl_ref.shape[1])):
        rates[j] = -jnp.exp(dl_ref[:, s]) * LOG2E


def widen(b_ref, c_ref, bw_ref, cw_ref, bd_ref):
    states, length = b_ref.shape
    for t in range(length):
        rows = slice(t * states, (t + 1) * states)
        bw_ref[rows, :] = jnp.broadcast_to(b_ref[:, t : t + 1], (states, LANES))
        cw_ref[rows, :] = jnp.broadcast_to(c_ref[:, t : t + 1], (states, LANES))
    n = lax.broadcasted_iota(jnp.int32, (states, BLOCK * states), 0)
    m = lax.broadcasted_iota(jnp.int32, (states, BLOCK * states), 1)
    repeat = jnp.where(n == m % states, 1.0, 0.0).astype(BF16)
    spread = lax.dot_general(b_ref[...].astype(BF16), repeat, (((0,), (0,)), ((), ())), preferred_element_type=F32)
    t = lax.broadcasted_iota(jnp.int32, (length, BLOCK * states), 0)
    m = lax.broadcasted_iota(jnp.int32, (length, BLOCK * states), 1)
    bd_ref[...] = jnp.where(t % BLOCK == m // states, spread, 0.0).astype(BF16)


def ends_kernel(x_ref, rim_ref, step_ref, dy_ref, b_ref, c_ref, cw_ref, cb_ref, sb_ref, dl_ref,
                out_ref, dls, dus, u_ref, sig_ref, slope_ref, dub_ref, bw_ref, cw2_ref, bd_ref,
                xe, dyf, rates):
    length, width = x_ref.shape
    states = dl_ref.shape[0]
    taps = cw_ref.shape[0]
    blocks = length // BLOCK
    weights = [cw_ref[k : k + 1, :] for k in range(taps)]
    bias, shift = cb_ref[...], sb_ref[...]
    slices = lane_slices(width)

    @pl.when(pl.program_id(0) == 0)
    def _():
        widen(b_ref, c_ref, bw_ref, cw2_ref, bd_ref)

    set_rates(dl_ref, rates)
    xe[0:8, :] = jnp.zeros((8, width), F32)
    xe[8 - (taps - 1) : 8, :] = rim_ref[...].astype(F32)
    total = jnp.zeros((8, width), F32)
    for b in range(blocks):
        rows = slice(b * BLOCK, (b + 1) * BLOCK)
        xe[8 + b * BLOCK : 8 + (b + 1) * BLOCK, :] = x_ref[rows, :].astype(F32)
        put(dyf, rows, dy_ref[rows, :].astype(F32))
        z = jnp.exp(step_ref[rows, :].astype(F32) + shift)
        series = z * (1.0 - z * (0.5 - z * (1.0 / 3.0 - 0.25 * z)))
        delta = jnp.where(z < 0.015625, series, jnp.log(1.0 + z))
        p = bias
        for k in range(taps):
            first = b * BLOCK + 9 - taps + k
            p = p + weights[k] * xe[first : first + BLOCK, :]
        gate = 1.0 / (1.0 + jnp.exp(-p))
        u = p * gate
        du = delta * u
        put(dls, rows, delta)
        put(dus, rows, du)
        u_ref[rows, :] = u
        sig_ref[rows, :] = z / (1.0 + z)
        slope_ref[rows, :] = gate + u * (1.0 - gate)
        dub_ref[rows, :] = du.astype(BF16)
        total = total + row_sum(delta)
    total = jnp.sum(total, axis=0, keepdims=True)

    def block(b, carry):
        state, decay, adjoint = (list(part) for part in carry)
        base = pl.multiple_of(b * BLOCK, BLOCK)
        for i in range(BLOCK):
            t = base + i
            rows = pl.ds(pl.multiple_of(t * states, states), states)
            b_column, c_column = bw_ref[rows, :], cw2_ref[rows, :]
            for j in range(len(slices)):
                a = jnp.exp2(row_of(dls, t, j) * rates[j])
                state[j] = a * state[j] + b_column * row_of(dus, t, j)
                decay[j] = decay[j] * a
                adjoint[j] = adjoint[j] + decay[j] * (c_column * row_of(dyf, t, j))
        return tuple(state), tuple(decay), tuple(adjoint)

    zero = tuple(jnp.zeros((states, LANES), F32) for _ in slices)
    one = tuple(jnp.ones((states, LANES), F32) for _ in slices)
    state, _, adjoint = lax.fori_loop(0, blocks, block, (zero, one, zero), unroll=blocks)
    for j, s in enumerate(slices):
        out_ref[0:states, s] = state[j].astype(BF16)
        out_ref[states : 2 * states, s] = adjoint[j].astype(BF16)
    high = total.astype(BF16)
    rest = total - high.astype(F32)
    middle = rest.astype(BF16)
    low = (rest - middle.astype(F32)).astype(BF16)
    row = lax.broadcasted_iota(jnp.int32, (16, width), 0)
    packed = jnp.where(row == 0, high.astype(F32), jnp.where(row == 1, middle.astype(F32), low.astype(F32)))
    out_ref[2 * states : 2 * states + 16, :] = packed.astype(BF16)


def main_kernel(si_ref, ai_ref, x_ref, rim_ref, dy_ref, dls, dus, u_ref, sig_ref, slope_ref, dub_ref,
                bb_ref, cb2_ref, bd_ref, cw_ref, dl_ref, sk_ref,
                gin_ref, borrow_ref, tail_ref, gb_ref, gc_ref, pg_ref,
                xe, dyf, ahs, hb, dpe, rates, naturals):
    length, width = x_ref.shape
    states = dl_ref.shape[0]
    taps = cw_ref.shape[0]
    blocks = length // BLOCK
    slices = lane_slices(width)
    tiles = range(len(slices))
    skip = sk_ref[...]

    @pl.when(pl.program_id(0) == 0)
    def _():
        gb_ref[...] = jnp.zeros_like(gb_ref)
        gc_ref[...] = jnp.zeros_like(gc_ref)

    set_rates(dl_ref, rates)
    for j, s in enumerate(slices):
        naturals[j] = (-jnp.exp(dl_ref[:, s])).astype(BF16)
    xe[0:8, :] = jnp.zeros((8, width), F32)
    xe[8 - (taps - 1) : 8, :] = rim_ref[...].astype(F32)
    for b in range(blocks):
        rows = slice(b * BLOCK, (b + 1) * BLOCK)
        xe[8 + b * BLOCK : 8 + (b + 1) * BLOCK, :] = x_ref[rows, :].astype(F32)
        put(dyf, rows, dy_ref[rows, :].astype(F32))
    dpe[0:8, :] = jnp.zeros((8, width), F32)
    dpe[length + 8 : length + 16, :] = jnp.zeros((8, width), F32)
    lane = lax.broadcasted_iota(jnp.int32, (states, length), 1)
    by_rows = (((1,), (1,)), ((), ()))

    def picked(table, product, b):
        for i in range(BLOCK):
            table = jnp.where(lane == b * BLOCK + i, product[i * states : (i + 1) * states], table)
        return table

    state = [si_ref[:, s] for s in slices]
    gc = jnp.zeros((states, length), F32)
    for b in range(blocks):
        for i in range(BLOCK):
            t = b * BLOCK + i
            rows = slice(t * states, (t + 1) * states)
            column = bb_ref[rows, :]
            for j in tiles:
                kept = jnp.exp2(row_of(dls, t, j) * rates[j]) * state[j]
                ahs[j, rows, :] = kept.astype(BF16)
                state[j] = kept + column * row_of(dus, t, j)
                hb[b % 2, j, i * states : (i + 1) * states, :] = state[j].astype(BF16)
        product = lax.dot_general(joined_tiles(hb.at[b % 2]), dy_ref[...], by_rows, preferred_element_type=F32)
        gc = picked(gc, product, b)
    gc_ref[...] += gc

    rows_of = lax.broadcasted_iota(jnp.int32, (BLOCK, BLOCK * states), 0)
    cols_of = lax.broadcasted_iota(jnp.int32, (BLOCK, BLOCK * states), 1)
    over_states = jnp.where(rows_of == cols_of // states, 1.0, 0.0).astype(BF16)
    rows_of = lax.broadcasted_iota(jnp.int32, (states, BLOCK * states), 0)
    cols_of = lax.broadcasted_iota(jnp.int32, (states, BLOCK * states), 1)
    over_steps = jnp.where(rows_of == cols_of % states, 1.0, 0.0).astype(BF16)

    adjoint = [ai_ref[:, s] for s in slices]
    gb = jnp.zeros((states, length), F32)
    rates_sum = [jnp.zeros((states, 2 * LANES), F32) for _ in range(0, len(slices), 2)]
    sums = [jnp.zeros((8, width), F32) for _ in range(taps + 3)]
    weights = [cw_ref[k : k + 1, :] for k in range(taps)]
    for b in reversed(range(blocks)):
        kept = {}
        for i in reversed(range(BLOCK)):
            t = b * BLOCK + i
            rows = slice(t * states, (t + 1) * states)
            column = cb2_ref[rows, :]
            for j in tiles:
                delta = row_of(dls, t, j)
                g = column * row_of(dyf, t, j) + adjoint[j]
                adjoint[j] = jnp.exp2(delta * rates[j]) * g
                low = g.astype(BF16)
                q = low * ahs[j, rows, :]
                kept[i, j] = low, q * naturals[j], q * delta.astype(BF16)

        def operand(m, which):
            return jnp.concatenate(
                [jnp.concatenate([kept[i, j][which] for i in range(BLOCK)], axis=0) for j in (2 * m, 2 * m + 1)],
                axis=1)

        rows = slice(b * BLOCK, (b + 1) * BLOCK)
        ddu, dwn, product = [], [], None
        for m in range(len(rates_sum)):
            g_block = operand(m, 0)
            ddu.append(jnp.dot(bd_ref[rows, :], g_block, preferred_element_type=F32))
            dwn.append(jnp.dot(over_states, operand(m, 1), preferred_element_type=F32))
            rates_sum[m] = rates_sum[m] + jnp.dot(over_steps, operand(m, 2), preferred_element_type=F32)
            part = lax.dot_general(g_block, dub_ref[:, 2 * m * LANES : 2 * (m + 1) * LANES], by_rows,
                                   preferred_element_type=F32)
            product = part if product is None else product + part
        gb = picked(gb, product, b)
        ddu, dwn = jnp.concatenate(ddu, axis=1), jnp.concatenate(dwn, axis=1)
        dy, u = take(dyf, rows), u_ref[rows, :]
        grad_v = (ddu * u + dwn) * sig_ref[rows, :]
        grad_p = (ddu * take(dls, rows) + skip * dy) * slope_ref[rows, :]
        dpe[8 + b * BLOCK : 8 + (b + 1) * BLOCK, :] = grad_p
        sums[taps] += row_sum(grad_p)
        sums[taps + 1] += row_sum(grad_v)
        sums[taps + 2] += row_sum(dy * u)
        grad_x = weights[taps - 1] * grad_p
        for k in range(taps):
            first = b * BLOCK + 9 - taps + k
            sums[k] += row_sum(grad_p * xe[first : first + BLOCK, :])
            if k < taps - 1:
                first = b * BLOCK + 7 + taps - k
                grad_x = grad_x + weights[k] * dpe[first : first + BLOCK, :]
        gin_ref[rows, :] = grad_x.astype(BF16)
        if b == blocks - 1:
            tail_ref[...] = grad_x
    gb_ref[...] += gb
    rates_sum = jnp.concatenate(rates_sum, axis=1)
    for j, s in enumerate(slices):
        pg_ref[0:states, s] = rates_sum[:, s] * (-jnp.exp(dl_ref[:, s]))
    grad_rim = weights[0] * dpe[taps - 1 : taps + 7, :]
    for k in range(1, taps):
        grad_rim = grad_rim + weights[k] * dpe[taps - 1 - k : taps + 7 - k, :]
    borrow_ref[...] = grad_rim[8 - borrow_ref.shape[0] : 8].astype(BF16)
    row = lax.broadcasted_iota(jnp.int32, (8, width), 0)
    packed = jnp.zeros((8, width), F32)
    for k in range(taps + 3):
        packed = jnp.where(row == k, jnp.sum(sums[k], axis=0, keepdims=True), packed)
    pg_ref[states : states + 8, :] = packed


def flipped(value, axis, bit):
    return lax.ppermute(value, axis, [(k, k ^ bit) for k in range(lax.axis_size(axis))])


def add_up(value):
    inner, outer = lax.axis_size("ctx"), lax.axis_size("dp")
    if inner & (inner - 1) or outer & (outer - 1):
        return lax.psum(value, ("dp", "ctx"))
    me = lax.axis_index("ctx")
    bits = [1 << k for k in range(inner.bit_length() - 1)]
    for bit in bits:
        half = value.shape[1] // 2
        upper = (me // bit) % 2
        give = lax.dynamic_slice_in_dim(value, (1 - upper) * half, half, 1)
        got = flipped(give, "ctx", bit)
        value = lax.dynamic_slice_in_dim(value, upper * half, half, 1) + got
    for k in range(outer.bit_length() - 1):
        value = value + flipped(value, "dp", 1 << k)
    for bit in reversed(bits):
        got = flipped(value, "ctx", bit)
        upper = (me // bit) % 2 == 1
        value = jnp.concatenate([jnp.where(upper, got, value), jnp.where(upper, value, got)], axis=1)
    return value


def entering(ends, decay_log):
    states = decay_log.shape[0]
    count, place = lax.axis_size("ctx"), lax.axis_index("ctx")
    rate = -jnp.exp(decay_log)

    def opened(piece):
        total = jnp.sum(piece[2 * states : 2 * states + 3].astype(F32), axis=0, keepdims=True)
        return piece[:states].astype(F32), piece[states : 2 * states].astype(F32), jnp.exp(rate * total)

    if count == 4:
        upper, late = place % 2 == 1, place // 2 == 1
        mine, other = opened(ends), opened(flipped(ends, "ctx", 1))
        pick = lambda a, b: jnp.where(upper, a, b)
        first, second = [pick(b, a) for a, b in zip(mine, other)], [pick(a, b) for a, b in zip(mine, other)]
        both = jnp.where(late, second[1] * first[2] + first[1], first[0] * second[2] + second[0])
        got = flipped(both.astype(BF16), "ctx", 2).astype(F32)
        before, after = jnp.where(late, got, 0.0), jnp.where(late, 0.0, got)
        state = jnp.where(upper, before * first[2] + first[0], before)
        adjoint = jnp.where(upper, after, after * second[2] + second[1])
        return state, adjoint
    gathered = lax.all_gather(ends, "ctx")
    state = adjoint = jnp.zeros(decay_log.shape, F32)
    for k in range(count - 1):
        end, _, decay = opened(gathered[k])
        state = jnp.where(k < place, decay * state + end, state)
    for k in range(count - 1, 0, -1):
        _, end, decay = opened(gathered[k])
        adjoint = jnp.where(k > place, decay * adjoint + end, adjoint)
    return state, adjoint


def whole(a):
    return pl.BlockSpec(a.shape, lambda i: (0,) * a.ndim)


def chunk(rows):
    return pl.BlockSpec((rows, WIDTH), lambda i: (0, i))


def tiled(length):
    return pl.BlockSpec((WIDTH // LANES, length, LANES), lambda i: (i, 0, 0))


def flat(a):
    return a.reshape(1, a.shape[0])


SHAPE = jax.ShapeDtypeStruct
PARAMS = pltpu.CompilerParams(vmem_limit_bytes=VMEM, dimension_semantics=("arbitrary",))


def call_ends(x, rims, step, dy, b_proj, c_proj, conv_weight, conv_bias, step_bias, decay_log):
    (length, channels), states = x.shape, decay_log.shape[0]
    taps, rim = conv_weight.shape[0], rims.shape[0]
    work = length * states * channels
    tiles = WIDTH // LANES
    long = SHAPE((channels // LANES, length, LANES), F32)
    plain = SHAPE((length, channels), F32)
    spread = [SHAPE((length * states, LANES), F32)] * 2 + [SHAPE((length, BLOCK * states), BF16)]
    return pl.pallas_call(
        ends_kernel,
        grid=(channels // WIDTH,),
        in_specs=[chunk(length), chunk(rim), chunk(length), chunk(length), whole(b_proj), whole(c_proj),
                  chunk(taps), chunk(1), chunk(1), chunk(states)],
        out_specs=[chunk(2 * states + 16)] + [tiled(length)] * 2 + [chunk(length)] * 4 + [whole(a) for a in spread],
        out_shape=[SHAPE((2 * states + 16, channels), BF16), long, long, plain, plain, plain,
                   SHAPE((length, channels), BF16)] + spread,
        scratch_shapes=[pltpu.VMEM((length + 16, WIDTH), F32),
                        pltpu.VMEM((tiles, length, LANES), F32),
                        pltpu.VMEM((tiles, states, LANES), F32)],
        compiler_params=PARAMS,
        cost_estimate=pl.CostEstimate(flops=8 * work, bytes_accessed=20 * length * channels, transcendentals=work),
    )(x, rims, step, dy, b_proj, c_proj, conv_weight, flat(conv_bias), flat(step_bias), decay_log)


def call_main(state_in, adjoint_in, x, rims, dy, saved, conv_weight, decay_log, skip_weight):
    (length, channels), states = x.shape, decay_log.shape[0]
    taps, rim = conv_weight.shape[0], rims.shape[0]
    work = length * states * channels
    tiles = WIDTH // LANES
    summed = pl.BlockSpec((states, length), lambda i: (0, 0))
    return pl.pallas_call(
        main_kernel,
        grid=(channels // WIDTH,),
        in_specs=[chunk(states), chunk(states), chunk(length), chunk(rim), chunk(length)] + [tiled(length)] * 2
        + [chunk(length)] * 4 + [whole(a) for a in saved[6:]] + [chunk(taps), chunk(states), chunk(1)],
        out_specs=[chunk(length), chunk(rim), chunk(BLOCK), summed, summed, chunk(states + 8)],
        out_shape=[SHAPE((length, channels), BF16), SHAPE((rim, channels), BF16), SHAPE((BLOCK, channels), F32),
                   SHAPE((states, length), F32), SHAPE((states, length), F32), SHAPE((states + 8, channels), F32)],
        scratch_shapes=[pltpu.VMEM((length + 16, WIDTH), F32),
                        pltpu.VMEM((tiles, length, LANES), F32),
                        pltpu.VMEM((tiles, length * states, LANES), BF16),
                        pltpu.VMEM((2, tiles, BLOCK * states, LANES), BF16),
                        pltpu.VMEM((length + 16, WIDTH), F32),
                        pltpu.VMEM((tiles, states, LANES), F32),
                        pltpu.VMEM((tiles, states, LANES), BF16)],
        compiler_params=PARAMS,
        cost_estimate=pl.CostEstimate(flops=20 * work, bytes_accessed=24 * length * channels, transcendentals=2 * work),
    )(state_in, adjoint_in, x, rims, dy, *saved, conv_weight, decay_log, flat(skip_weight))


def per_device(scan_input, step_raw, input_proj, output_proj, out_cotangent, conv_weight, conv_bias, step_bias,
               decay_log, skip_weight):
    documents, length, channels = scan_input.shape
    states, taps = decay_log.shape[0], conv_weight.shape[0]
    rim = taps - 1
    count = lax.axis_size("ctx")
    forth = [(k, k + 1) for k in range(count - 1)]
    back = [(k + 1, k) for k in range(count - 1)]

    def one(x, step, b_proj, c_proj, dy):
        rims = lax.ppermute(x[length - rim :, :], "ctx", forth)
        ends, *saved = call_ends(x, rims, step, dy, b_proj, c_proj, conv_weight, conv_bias, step_bias, decay_log)
        state_in, adjoint_in = entering(ends, decay_log)
        return call_main(state_in, adjoint_in, x, rims, dy, saved, conv_weight, decay_log, skip_weight)

    outs = []
    for d in range(documents):
        gin, borrow, tail, gb, gc, sums = one(
            scan_input[d], step_raw[d], input_proj[d], output_proj[d], out_cotangent[d])
        given = lax.ppermute(borrow, "ctx", back).astype(F32)
        tail = (tail + jnp.pad(given, ((BLOCK - rim, 0), (0, 0)))).astype(BF16)
        gin = lax.dynamic_update_slice(gin, tail, (length - BLOCK, 0))
        outs.append((gin, gb, gc, sums))
    sums = add_up(sum(o[3] for o in outs))
    return (
        jnp.stack([o[0] for o in outs]),
        jnp.stack([o[1] for o in outs]),
        jnp.stack([o[2] for o in outs]),
        sums[states : states + taps],
        sums[states + taps],
        sums[states + taps + 1],
        sums[:states],
        sums[states + taps + 2],
    )


def solution(mesh):
    split, columns = P("dp", "ctx", None), P("dp", None, "ctx")
    return jax.shard_map(
        per_device,
        mesh=mesh,
        in_specs=(split, split, columns, columns, split, P(), P(), P(), P(), P()),
        out_specs=(split, columns, columns, P(), P(), P(), P(), P()),
        check_vma=False,
    )
```

```python
import math
from functools import partial

import jax
import jax.numpy as jnp
from jax import lax
from jax.experimental import pallas as pl
from jax.experimental.pallas import tpu as pltpu
from jax.sharding import PartitionSpec as P

F32 = jnp.float32
BF16 = jnp.bfloat16
LOG2E = 1.0 / math.log(2.0)
BLOCK = 16
LANES = 128
WIDTH = 512
ENDS_WIDTH = 1024
VMEM = 60 * 1024 * 1024


def lane_slices(width):
    return [slice(j, j + LANES) for j in range(0, width, LANES)]


def row_of(ref, t, j):
    row = ref[j, pl.ds(t, 8, stride=0), :]
    return jnp.concatenate([row, row], axis=0)


def put(ref, rows, value):
    for j in range(ref.shape[0]):
        ref[j, rows, :] = value[:, j * LANES : (j + 1) * LANES]


def take(ref, rows):
    return jnp.concatenate([ref[j, rows, :] for j in range(ref.shape[0])], axis=1)


def joined_tiles(ref):
    return jnp.concatenate([ref[j] for j in range(ref.shape[0])], axis=1)


def row_sum(value):
    total = value[0:8]
    for r in range(8, value.shape[0], 8):
        total = total + value[r : r + 8]
    return total


def set_rates(dl_ref, rates):
    for j, s in enumerate(lane_slices(dl_ref.shape[1])):
        rates[j] = -jnp.exp(dl_ref[:, s]) * LOG2E


def widen(b_ref, c_ref, bw_ref, cw_ref, bd_ref):
    states, length = b_ref.shape
    for t in range(length):
        rows = slice(t * states, (t + 1) * states)
        bw_ref[rows, :] = jnp.broadcast_to(b_ref[:, t : t + 1], (states, LANES))
        cw_ref[rows, :] = jnp.broadcast_to(c_ref[:, t : t + 1], (states, LANES))
    n = lax.broadcasted_iota(jnp.int32, (states, BLOCK * states), 0)
    m = lax.broadcasted_iota(jnp.int32, (states, BLOCK * states), 1)
    repeat = jnp.where(n == m % states, 1.0, 0.0).astype(BF16)
    spread = lax.dot_general(b_ref[...].astype(BF16), repeat, (((0,), (0,)), ((), ())), preferred_element_type=F32)
    t = lax.broadcasted_iota(jnp.int32, (length, BLOCK * states), 0)
    m = lax.broadcasted_iota(jnp.int32, (length, BLOCK * states), 1)
    bd_ref[...] = jnp.where(t % BLOCK == m // states, spread, 0.0).astype(BF16)


def low_parts(value):
    high = value.astype(BF16)
    return high, (value - high.astype(F32)).astype(BF16)


def summed_over(mask, value):
    high, low = low_parts(value)
    mask = jnp.where(mask, 1.0, 0.0).astype(BF16)
    return jnp.dot(mask, high, preferred_element_type=F32) + jnp.dot(mask, low, preferred_element_type=F32)


def set_diagonals(proj_ref, diag):
    states, length = proj_ref.shape
    n = lax.broadcasted_iota(jnp.int32, (BLOCK, BLOCK * states), 0)
    m = lax.broadcasted_iota(jnp.int32, (BLOCK, BLOCK * states), 1)
    repeat = jnp.where(n == m // states, 1.0, 0.0).astype(BF16)
    n = lax.broadcasted_iota(jnp.int32, (states, BLOCK * states), 0)
    m = lax.broadcasted_iota(jnp.int32, (states, BLOCK * states), 1)
    for b in range(length // BLOCK):
        columns = proj_ref[:, b * BLOCK : (b + 1) * BLOCK].astype(BF16)
        spread = jnp.dot(columns, repeat, preferred_element_type=F32)
        diag[b] = jnp.where(n == m % states, spread, 0.0).astype(BF16)


def decayed_sum(exponents, weights, diag, rates, width):
    blocks, states = diag.shape[0], diag.shape[1]
    tiles = width // LANES
    total = [jnp.zeros((states, 2 * LANES), F32) for _ in range(0, tiles, 2)]
    for b in range(blocks):
        for m in range(len(total)):
            columns = []
            for j in (2 * m, 2 * m + 1):
                terms = []
                for i in range(BLOCK):
                    t = b * BLOCK + i
                    decay = jnp.exp2(row_of(exponents, t, j).astype(BF16) * rates[j])
                    terms.append(decay * row_of(weights, t, j).astype(BF16))
                columns.append(jnp.concatenate(terms, axis=0))
            total[m] = total[m] + jnp.dot(diag[b], jnp.concatenate(columns, axis=1), preferred_element_type=F32)
    return jnp.concatenate(total, axis=1)


def ends_kernel(late_ref, x_ref, rim_ref, step_ref, dy_ref, b_ref, c_ref, cw_ref, cb_ref, sb_ref, dl_ref,
                ends_ref, far_ref, dls, sig_ref, dus, u_ref, slope_ref, dub_ref,
                xe, dyf, upto, after, b_diag, c_diag, rates):
    length, width = x_ref.shape
    states, taps = dl_ref.shape[0], cw_ref.shape[0]
    weights = [cw_ref[k : k + 1, :] for k in range(taps)]
    bias, shift = cb_ref[...], sb_ref[...]

    @pl.when(pl.program_id(0) == 0)
    def _():
        set_diagonals(b_ref, b_diag)
        set_diagonals(c_ref, c_diag)

    for j, s in enumerate(lane_slices(width)):
        rates[j] = (-jnp.exp(dl_ref[:, s]) * LOG2E).astype(BF16)
    xe[0:8, :] = jnp.zeros((8, width), F32)
    xe[8 - (taps - 1) : 8, :] = rim_ref[...].astype(F32)
    for b in range(length // BLOCK):
        rows = slice(b * BLOCK, (b + 1) * BLOCK)
        xe[8 + b * BLOCK : 8 + (b + 1) * BLOCK, :] = x_ref[rows, :].astype(F32)
        put(dyf, rows, dy_ref[rows, :].astype(F32))
        z = jnp.exp(step_ref[rows, :].astype(F32) + shift)
        series = z * (1.0 - z * (0.5 - z * (1.0 / 3.0 - 0.25 * z)))
        delta = jnp.where(z < 0.015625, series, jnp.log(1.0 + z))
        p = bias
        for k in range(taps):
            first = b * BLOCK + 9 - taps + k
            p = p + weights[k] * xe[first : first + BLOCK, :]
        gate = 1.0 / (1.0 + jnp.exp(-p))
        u = p * gate
        du = delta * u
        put(dls, rows, delta)
        put(dus, rows, du)
        sig_ref[rows, :] = z / (1.0 + z)
        u_ref[rows, :] = u
        slope_ref[rows, :] = gate + u * (1.0 - gate)
        dub_ref[rows, :] = du.astype(BF16)
    t = lax.broadcasted_iota(jnp.int32, (length, length), 0)
    r = lax.broadcasted_iota(jnp.int32, (length, length), 1)
    for j in range(width // LANES):
        upto[j] = summed_over(r <= t, dls[j])
        after[j] = summed_over(r > t, dls[j])
    adjoint = decayed_sum(upto, dyf, c_diag, rates, width)
    state = decayed_sum(after, dus, b_diag, rates, width)
    total = take(after, slice(0, 1)) + take(dls, slice(0, 1))
    high = total.astype(BF16)
    middle = (total - high.astype(F32)).astype(BF16)
    low = (total - high.astype(F32) - middle.astype(F32)).astype(BF16)
    row = lax.broadcasted_iota(jnp.int32, (16, width), 0)
    packed = jnp.where(row == 0, high.astype(F32), jnp.where(row == 1, middle.astype(F32), low.astype(F32)))
    packed = packed.astype(BF16)
    ends_ref[0:states, :] = state.astype(BF16)
    ends_ref[states : 2 * states, :] = adjoint.astype(BF16)
    ends_ref[2 * states : 2 * states + 16, :] = packed
    far_ref[0:states, :] = jnp.where(late_ref[0] == 1, adjoint, state).astype(BF16)
    far_ref[states : states + 16, :] = packed


def joined(place_ref, sib_ref, far_ref, far_sib_ref, rate, s):
    late, upper = place_ref[0] >= 2, place_ref[0] % 2 == 1
    states = rate.shape[0]

    def decay(ref, first):
        parts = ref[first : first + 16, s].astype(F32)
        return jnp.exp2(rate * (parts[0:1] + parts[1:2] + parts[2:3]))

    pieces = [(ref[0:states, s].astype(F32), decay(ref, states)) for ref in (far_ref, far_sib_ref)]
    first = [jnp.where(upper, b, a) for a, b in zip(*pieces)]
    second = [jnp.where(upper, a, b) for a, b in zip(*pieces)]
    far = jnp.where(late, second[1] * first[0] + second[0], first[0] + first[1] * second[0])
    step = decay(sib_ref, 2 * states) * far
    sib_state, sib_adjoint = sib_ref[0:states, s].astype(F32), sib_ref[states : 2 * states, s].astype(F32)
    state = jnp.where(late, far, 0.0)
    state = jnp.where(upper, sib_state + jnp.where(late, step, 0.0), state)
    adjoint = jnp.where(late, 0.0, far)
    adjoint = jnp.where(upper, adjoint, sib_adjoint + jnp.where(late, 0.0, step))
    return state, adjoint


def main_kernel(entering, place_ref, *refs):
    (x_ref, rim_ref, dy_ref, dls, sig_ref, dus, u_ref, slope_ref, dub_ref, b_ref, c_ref, cw_ref, dl_ref, sk_ref,
     gin_ref, borrow_ref, tail_ref, gb_ref, gc_ref, pg_ref,
     xe, dyf, ahs, hb, dpe, rates, naturals, bb_ref, cb2_ref, bd_ref, back) = refs[entering:]
    length, width = x_ref.shape
    states = dl_ref.shape[0]
    taps = cw_ref.shape[0]
    blocks = length // BLOCK
    slices = lane_slices(width)
    tiles = range(len(slices))
    skip = sk_ref[...]

    @pl.when(pl.program_id(0) == 0)
    def _():
        gb_ref[...] = jnp.zeros_like(gb_ref)
        gc_ref[...] = jnp.zeros_like(gc_ref)
        widen(b_ref, c_ref, bb_ref, cb2_ref, bd_ref)

    set_rates(dl_ref, rates)
    for j, s in enumerate(slices):
        naturals[j] = (-jnp.exp(dl_ref[:, s])).astype(BF16)
    xe[0:8, :] = jnp.zeros((8, width), F32)
    xe[8 - (taps - 1) : 8, :] = rim_ref[...].astype(F32)
    for b in range(blocks):
        rows = slice(b * BLOCK, (b + 1) * BLOCK)
        xe[8 + b * BLOCK : 8 + (b + 1) * BLOCK, :] = x_ref[rows, :].astype(F32)
        put(dyf, rows, dy_ref[rows, :].astype(F32))
    dpe[0:8, :] = jnp.zeros((8, width), F32)
    dpe[length + 8 : length + 16, :] = jnp.zeros((8, width), F32)
    lane = lax.broadcasted_iota(jnp.int32, (states, length), 1)
    by_rows = (((1,), (1,)), ((), ()))

    def picked(table, product, b):
        for i in range(BLOCK):
            table = jnp.where(lane == b * BLOCK + i, product[i * states : (i + 1) * states], table)
        return table

    if entering == 2:
        state, adjoint = ([ref[:, s] for s in slices] for ref in refs[:2])
    else:
        state, adjoint = zip(*(joined(place_ref, *refs[:3], rates[j], s) for j, s in enumerate(slices)))
        state, adjoint = list(state), list(adjoint)
    for j in tiles:
        back[j] = adjoint[j]
    gc = jnp.zeros((states, length), F32)
    for b in range(blocks):
        for i in range(BLOCK):
            t = b * BLOCK + i
            rows = slice(t * states, (t + 1) * states)
            column = bb_ref[rows, :]
            for j in tiles:
                kept = jnp.exp2(row_of(dls, t, j) * rates[j]) * state[j]
                ahs[j, rows, :] = kept.astype(BF16)
                state[j] = kept + column * row_of(dus, t, j)
                hb[b % 2, j, i * states : (i + 1) * states, :] = state[j].astype(BF16)
        product = lax.dot_general(joined_tiles(hb.at[b % 2]), dy_ref[...], by_rows, preferred_element_type=F32)
        gc = picked(gc, product, b)
    gc_ref[...] += gc

    rows_of = lax.broadcasted_iota(jnp.int32, (BLOCK, BLOCK * states), 0)
    cols_of = lax.broadcasted_iota(jnp.int32, (BLOCK, BLOCK * states), 1)
    over_states = jnp.where(rows_of == cols_of // states, 1.0, 0.0).astype(BF16)
    rows_of = lax.broadcasted_iota(jnp.int32, (states, BLOCK * states), 0)
    cols_of = lax.broadcasted_iota(jnp.int32, (states, BLOCK * states), 1)
    over_steps = jnp.where(rows_of == cols_of % states, 1.0, 0.0).astype(BF16)

    adjoint = [back[j] for j in tiles]
    gb = jnp.zeros((states, length), F32)
    rates_sum = [jnp.zeros((states, 2 * LANES), F32) for _ in range(0, len(slices), 2)]
    sums = [jnp.zeros((8, width), F32) for _ in range(taps + 3)]
    weights = [cw_ref[k : k + 1, :] for k in range(taps)]
    for b in reversed(range(blocks)):
        kept = {}
        for i in reversed(range(BLOCK)):
            t = b * BLOCK + i
            rows = slice(t * states, (t + 1) * states)
            column = cb2_ref[rows, :]
            for j in tiles:
                delta = row_of(dls, t, j)
                g = column * row_of(dyf, t, j) + adjoint[j]
                adjoint[j] = jnp.exp2(delta * rates[j]) * g
                low = g.astype(BF16)
                q = low * ahs[j, rows, :]
                kept[i, j] = low, q * naturals[j], q * delta.astype(BF16)

        def operand(m, which):
            return jnp.concatenate(
                [jnp.concatenate([kept[i, j][which] for i in range(BLOCK)], axis=0) for j in (2 * m, 2 * m + 1)],
                axis=1)

        rows = slice(b * BLOCK, (b + 1) * BLOCK)
        ddu, dwn, product = [], [], None
        for m in range(len(rates_sum)):
            g_block = operand(m, 0)
            ddu.append(jnp.dot(bd_ref[rows, :], g_block, preferred_element_type=F32))
            dwn.append(jnp.dot(over_states, operand(m, 1), preferred_element_type=F32))
            rates_sum[m] = rates_sum[m] + jnp.dot(over_steps, operand(m, 2), preferred_element_type=F32)
            part = lax.dot_general(g_block, dub_ref[:, 2 * m * LANES : 2 * (m + 1) * LANES], by_rows,
                                   preferred_element_type=F32)
            product = part if product is None else product + part
        gb = picked(gb, product, b)
        ddu, dwn = jnp.concatenate(ddu, axis=1), jnp.concatenate(dwn, axis=1)
        dy, u = take(dyf, rows), u_ref[rows, :]
        grad_v = (ddu * u + dwn) * sig_ref[rows, :]
        grad_p = (ddu * take(dls, rows) + skip * dy) * slope_ref[rows, :]
        dpe[8 + b * BLOCK : 8 + (b + 1) * BLOCK, :] = grad_p
        sums[taps] += row_sum(grad_p)
        sums[taps + 1] += row_sum(grad_v)
        sums[taps + 2] += row_sum(dy * u)
        grad_x = weights[taps - 1] * grad_p
        for k in range(taps):
            first = b * BLOCK + 9 - taps + k
            sums[k] += row_sum(grad_p * xe[first : first + BLOCK, :])
            if k < taps - 1:
                first = b * BLOCK + 7 + taps - k
                grad_x = grad_x + weights[k] * dpe[first : first + BLOCK, :]
        gin_ref[rows, :] = grad_x.astype(BF16)
        if b == blocks - 1:
            tail_ref[...] = grad_x
    gb_ref[...] += gb
    rates_sum = jnp.concatenate(rates_sum, axis=1)
    for j, s in enumerate(slices):
        pg_ref[0:states, s] = rates_sum[:, s] * (-jnp.exp(dl_ref[:, s]))
    grad_rim = weights[0] * dpe[taps - 1 : taps + 7, :]
    for k in range(1, taps):
        grad_rim = grad_rim + weights[k] * dpe[taps - 1 - k : taps + 7 - k, :]
    borrow_ref[...] = grad_rim[8 - borrow_ref.shape[0] : 8].astype(BF16)
    row = lax.broadcasted_iota(jnp.int32, (8, width), 0)
    packed = jnp.zeros((8, width), F32)
    for k in range(taps + 3):
        packed = jnp.where(row == k, jnp.sum(sums[k], axis=0, keepdims=True), packed)
    pg_ref[states : states + 8, :] = packed


def flipped(value, axis, bit):
    return lax.ppermute(value, axis, [(k, k ^ bit) for k in range(lax.axis_size(axis))])


def add_up(value):
    inner, outer = lax.axis_size("ctx"), lax.axis_size("dp")
    if inner & (inner - 1) or outer & (outer - 1):
        return lax.psum(value, ("dp", "ctx"))
    me = lax.axis_index("ctx")
    bits = [1 << k for k in range(inner.bit_length() - 1)]
    for bit in bits:
        half = value.shape[1] // 2
        upper = (me // bit) % 2
        give = lax.dynamic_slice_in_dim(value, (1 - upper) * half, half, 1)
        got = flipped(give, "ctx", bit)
        value = lax.dynamic_slice_in_dim(value, upper * half, half, 1) + got
    for k in range(outer.bit_length() - 1):
        value = value + flipped(value, "dp", 1 << k)
    for bit in reversed(bits):
        got = flipped(value, "ctx", bit)
        upper = (me // bit) % 2 == 1
        value = jnp.concatenate([jnp.where(upper, got, value), jnp.where(upper, value, got)], axis=1)
    return value


def entering(ends, far, decay_log):
    states = decay_log.shape[0]
    count, place = lax.axis_size("ctx"), lax.axis_index("ctx")
    if count == 4:
        far = flipped(far, "ctx", 2)
        return flipped(ends, "ctx", 1), far, flipped(far, "ctx", 1)
    rate = -jnp.exp(decay_log)
    gathered = lax.all_gather(ends, "ctx").astype(F32)
    total = gathered[:, 2 * states] + gathered[:, 2 * states + 1] + gathered[:, 2 * states + 2]
    decay = jnp.exp(rate[None] * total[:, None, :])
    state = adjoint = jnp.zeros(decay_log.shape, F32)
    for k in range(count - 1):
        state = jnp.where(k < place, decay[k] * state + gathered[k, :states], state)
    for k in range(count - 1, 0, -1):
        adjoint = jnp.where(k > place, decay[k] * adjoint + gathered[k, states : 2 * states], adjoint)
    return state, adjoint


def whole(a):
    return pl.BlockSpec(a.shape, lambda i, *_: (0,) * a.ndim)


def chunk(rows):
    return pl.BlockSpec((rows, WIDTH), lambda i, *_: (0, i))


def tiled(length):
    return pl.BlockSpec((WIDTH // LANES, length, LANES), lambda i, *_: (i, 0, 0))


def flat(a):
    return a.reshape(1, a.shape[0])


SHAPE = jax.ShapeDtypeStruct
PARAMS = pltpu.CompilerParams(vmem_limit_bytes=VMEM, dimension_semantics=("arbitrary",))


def call_ends(late, x, rims, step, dy, b_proj, c_proj, conv_weight, conv_bias, step_bias, decay_log):
    (length, channels), states = x.shape, decay_log.shape[0]
    taps, rim = conv_weight.shape[0], rims.shape[0]
    work = length * states * channels
    tiles = ENDS_WIDTH // LANES
    plain = SHAPE((length, channels), F32)
    long = SHAPE((channels // LANES, length, LANES), F32)
    chunk = lambda rows: pl.BlockSpec((rows, ENDS_WIDTH), lambda i, *_: (0, i))
    tiled = pl.BlockSpec((tiles, length, LANES), lambda i, *_: (i, 0, 0))
    diag = pltpu.VMEM((length // BLOCK, states, BLOCK * states), BF16)
    return pl.pallas_call(
        ends_kernel,
        grid_spec=pltpu.PrefetchScalarGridSpec(
            num_scalar_prefetch=1,
            grid=(channels // ENDS_WIDTH,),
            in_specs=[chunk(length), chunk(rim), chunk(length), chunk(length), whole(b_proj), whole(c_proj),
                      chunk(taps), chunk(1), chunk(1), chunk(states)],
            out_specs=[chunk(2 * states + 16), chunk(states + 16), tiled, chunk(length), tiled] + [chunk(length)] * 3,
            scratch_shapes=[pltpu.VMEM((length + 16, ENDS_WIDTH), F32)] + [pltpu.VMEM((tiles, length, LANES), F32)] * 3
            + [diag, diag, pltpu.VMEM((tiles, states, LANES), BF16)],
        ),
        out_shape=[SHAPE((2 * states + 16, channels), BF16), SHAPE((states + 16, channels), BF16), long, plain, long,
                   plain, plain, SHAPE((length, channels), BF16)],
        compiler_params=PARAMS,
        cost_estimate=pl.CostEstimate(flops=8 * work, bytes_accessed=30 * length * channels, transcendentals=work),
    )(late, x, rims, step, dy, b_proj, c_proj, conv_weight, flat(conv_bias), flat(step_bias), decay_log)


def call_main(place, entering, x, rims, dy, saved, b_proj, c_proj, conv_weight, decay_log, skip_weight):
    (length, channels), states = x.shape, decay_log.shape[0]
    taps, rim = conv_weight.shape[0], rims.shape[0]
    work = length * states * channels
    tiles = WIDTH // LANES
    summed = pl.BlockSpec((states, length), lambda i, *_: (0, 0))
    return pl.pallas_call(
        partial(main_kernel, len(entering)),
        grid_spec=pltpu.PrefetchScalarGridSpec(
            num_scalar_prefetch=1,
            grid=(channels // WIDTH,),
            in_specs=[chunk(a.shape[0]) for a in entering] + [chunk(length), chunk(rim), chunk(length), tiled(length),
                      chunk(length), tiled(length)] + [chunk(length)] * 3 + [whole(b_proj), whole(c_proj), chunk(taps),
                      chunk(states), chunk(1)],
            out_specs=[chunk(length), chunk(rim), chunk(BLOCK), summed, summed, chunk(states + 8)],
            scratch_shapes=[pltpu.VMEM((length + 16, WIDTH), F32),
                            pltpu.VMEM((tiles, length, LANES), F32),
                            pltpu.VMEM((tiles, length * states, LANES), BF16),
                            pltpu.VMEM((2, tiles, BLOCK * states, LANES), BF16),
                            pltpu.VMEM((length + 16, WIDTH), F32),
                            pltpu.VMEM((tiles, states, LANES), F32),
                            pltpu.VMEM((tiles, states, LANES), BF16),
                            pltpu.VMEM((length * states, LANES), F32),
                            pltpu.VMEM((length * states, LANES), F32),
                            pltpu.VMEM((length, BLOCK * states), BF16),
                            pltpu.VMEM((tiles, states, LANES), F32)],
        ),
        out_shape=[SHAPE((length, channels), BF16), SHAPE((rim, channels), BF16), SHAPE((BLOCK, channels), F32),
                   SHAPE((states, length), F32), SHAPE((states, length), F32), SHAPE((states + 8, channels), F32)],
        compiler_params=PARAMS,
        cost_estimate=pl.CostEstimate(flops=20 * work, bytes_accessed=24 * length * channels, transcendentals=2 * work),
    )(place, *entering, x, rims, dy, *saved, b_proj, c_proj, conv_weight, decay_log, flat(skip_weight))


def per_device(scan_input, step_raw, input_proj, output_proj, out_cotangent, conv_weight, conv_bias, step_bias,
               decay_log, skip_weight):
    documents, length, channels = scan_input.shape
    states, taps = decay_log.shape[0], conv_weight.shape[0]
    rim = taps - 1
    count = lax.axis_size("ctx")
    place = lax.axis_index("ctx").astype(jnp.int32).reshape(1)
    late = (place >= count // 2).astype(jnp.int32)
    forth = [(k, k + 1) for k in range(count - 1)]
    back = [(k + 1, k) for k in range(count - 1)]

    def one(x, step, b_proj, c_proj, dy):
        rims = lax.ppermute(x[length - rim :, :], "ctx", forth)
        ends, far, *saved = call_ends(late, x, rims, step, dy, b_proj, c_proj, conv_weight, conv_bias, step_bias,
                                      decay_log)
        return call_main(place, entering(ends, far, decay_log), x, rims, dy, saved, b_proj, c_proj,
                         conv_weight, decay_log, skip_weight)

    outs = []
    for d in range(documents):
        gin, borrow, tail, gb, gc, sums = one(
            scan_input[d], step_raw[d], input_proj[d], output_proj[d], out_cotangent[d])
        given = lax.ppermute(borrow, "ctx", back).astype(F32)
        tail = (tail + jnp.pad(given, ((BLOCK - rim, 0), (0, 0)))).astype(BF16)
        gin = lax.dynamic_update_slice(gin, tail, (length - BLOCK, 0))
        outs.append((gin, gb, gc, sums))
    sums = add_up(sum(o[3] for o in outs))
    return (
        jnp.stack([o[0] for o in outs]),
        jnp.stack([o[1] for o in outs]),
        jnp.stack([o[2] for o in outs]),
        sums[states : states + taps],
        sums[states + taps],
        sums[states + taps + 1],
        sums[:states],
        sums[states + taps + 2],
    )


def solution(mesh):
    split, columns = P("dp", "ctx", None), P("dp", None, "ctx")
    return jax.shard_map(
        per_device,
        mesh=mesh,
        in_specs=(split, split, columns, columns, split, P(), P(), P(), P(), P()),
        out_specs=(split, columns, columns, P(), P(), P(), P(), P()),
        check_vma=False,
    )
```

```python
import math
from functools import partial

import jax
import jax.numpy as jnp
from jax import lax
from jax.experimental import pallas as pl
from jax.experimental.pallas import tpu as pltpu
from jax.sharding import PartitionSpec as P

F32 = jnp.float32
BF16 = jnp.bfloat16
LOG2E = 1.0 / math.log(2.0)
BLOCK = 16
LANES = 128
WIDTH = 512
ENDS_WIDTH = 1024
VMEM = 60 * 1024 * 1024


def lane_slices(width):
    return [slice(j, j + LANES) for j in range(0, width, LANES)]


def row_of(ref, t, j):
    row = ref[j, pl.ds(t, 8, stride=0), :]
    return jnp.concatenate([row, row], axis=0)


def put(ref, rows, value):
    for j in range(ref.shape[0]):
        ref[j, rows, :] = value[:, j * LANES : (j + 1) * LANES]


def take(ref, rows):
    return jnp.concatenate([ref[j, rows, :] for j in range(ref.shape[0])], axis=1)


def joined_tiles(ref):
    return jnp.concatenate([ref[j] for j in range(ref.shape[0])], axis=1)


def row_sum(value):
    total = value[0:8]
    for r in range(8, value.shape[0], 8):
        total = total + value[r : r + 8]
    return total


def set_rates(dl_ref, rates):
    for j, s in enumerate(lane_slices(dl_ref.shape[1])):
        rates[j] = -jnp.exp(dl_ref[:, s]) * LOG2E


def widen(b_ref, c_ref, bw_ref, cw_ref, bd_ref):
    states, length = b_ref.shape
    for t in range(length):
        rows = slice(t * states, (t + 1) * states)
        bw_ref[rows, :] = jnp.broadcast_to(b_ref[:, t : t + 1], (states, LANES))
        cw_ref[rows, :] = jnp.broadcast_to(c_ref[:, t : t + 1], (states, LANES))
    n = lax.broadcasted_iota(jnp.int32, (states, BLOCK * states), 0)
    m = lax.broadcasted_iota(jnp.int32, (states, BLOCK * states), 1)
    repeat = jnp.where(n == m % states, 1.0, 0.0).astype(BF16)
    spread = lax.dot_general(b_ref[...].astype(BF16), repeat, (((0,), (0,)), ((), ())), preferred_element_type=F32)
    t = lax.broadcasted_iota(jnp.int32, (length, BLOCK * states), 0)
    m = lax.broadcasted_iota(jnp.int32, (length, BLOCK * states), 1)
    bd_ref[...] = jnp.where(t % BLOCK == m // states, spread, 0.0).astype(BF16)


def set_diagonals(proj_ref, diag):
    states, length = proj_ref.shape
    n = lax.broadcasted_iota(jnp.int32, (BLOCK, BLOCK * states), 0)
    m = lax.broadcasted_iota(jnp.int32, (BLOCK, BLOCK * states), 1)
    repeat = jnp.where(n == m // states, 1.0, 0.0).astype(BF16)
    n = lax.broadcasted_iota(jnp.int32, (states, BLOCK * states), 0)
    m = lax.broadcasted_iota(jnp.int32, (states, BLOCK * states), 1)
    for b in range(length // BLOCK):
        columns = proj_ref[:, b * BLOCK : (b + 1) * BLOCK].astype(BF16)
        spread = jnp.dot(columns, repeat, preferred_element_type=F32)
        diag[b] = jnp.where(n == m % states, spread, 0.0).astype(BF16)


def piece_ends(steps, inputs, outputs, b_wide, c_diag, rates, width):
    blocks, states = c_diag.shape[0], c_diag.shape[1]
    tiles = range(width // LANES)
    state = [jnp.zeros((states, LANES), F32) for _ in tiles]
    decay = [jnp.ones((states, LANES), F32) for _ in tiles]
    adjoint = [jnp.zeros((states, 2 * LANES), F32) for _ in tiles[::2]]
    for b in range(blocks):
        terms = [[] for _ in tiles]
        for i in range(BLOCK):
            t = b * BLOCK + i
            column = b_wide[t * states : (t + 1) * states, :]
            for j in tiles:
                a = jnp.exp2(row_of(steps, t, j) * rates[j])
                state[j] = a * state[j] + column * row_of(inputs, t, j)
                decay[j] = decay[j] * a
                terms[j].append((decay[j] * row_of(outputs, t, j)).astype(BF16))
        for m in range(len(adjoint)):
            pair = [jnp.concatenate(terms[j], axis=0) for j in (2 * m, 2 * m + 1)]
            adjoint[m] = adjoint[m] + jnp.dot(c_diag[b], jnp.concatenate(pair, axis=1), preferred_element_type=F32)
    return jnp.concatenate(state, axis=1), jnp.concatenate(adjoint, axis=1)


def ends_kernel(x_ref, rim_ref, step_ref, dy_ref, b_ref, c_ref, cw_ref, cb_ref, sb_ref, dl_ref,
                ends_ref, dls, sig_ref, dus, u_ref, slope_ref, dub_ref,
                xe, dyf, b_wide, c_diag, rates):
    length, width = x_ref.shape
    states, taps = dl_ref.shape[0], cw_ref.shape[0]
    weights = [cw_ref[k : k + 1, :] for k in range(taps)]
    bias, shift = cb_ref[...], sb_ref[...]

    @pl.when(pl.program_id(0) == 0)
    def _():
        for t in range(length):
            b_wide[t * states : (t + 1) * states, :] = jnp.broadcast_to(b_ref[:, t : t + 1], (states, LANES))
        set_diagonals(c_ref, c_diag)

    set_rates(dl_ref, rates)
    total = jnp.zeros((8, width), F32)
    xe[0:8, :] = jnp.zeros((8, width), F32)
    xe[8 - (taps - 1) : 8, :] = rim_ref[...].astype(F32)
    for b in range(length // BLOCK):
        rows = slice(b * BLOCK, (b + 1) * BLOCK)
        xe[8 + b * BLOCK : 8 + (b + 1) * BLOCK, :] = x_ref[rows, :].astype(F32)
        put(dyf, rows, dy_ref[rows, :].astype(F32))
        z = jnp.exp(step_ref[rows, :].astype(F32) + shift)
        series = z * (1.0 - z * (0.5 - z * (1.0 / 3.0 - 0.25 * z)))
        delta = jnp.where(z < 0.015625, series, jnp.log(1.0 + z))
        p = bias
        for k in range(taps):
            first = b * BLOCK + 9 - taps + k
            p = p + weights[k] * xe[first : first + BLOCK, :]
        gate = 1.0 / (1.0 + jnp.exp(-p))
        u = p * gate
        du = delta * u
        put(dls, rows, delta)
        put(dus, rows, du)
        sig_ref[rows, :] = z / (1.0 + z)
        u_ref[rows, :] = u
        slope_ref[rows, :] = gate + u * (1.0 - gate)
        dub_ref[rows, :] = du.astype(BF16)
        total = total + row_sum(delta)
    state, adjoint = piece_ends(dls, dus, dyf, b_wide, c_diag, rates, width)
    total = jnp.sum(total, axis=0, keepdims=True)
    high = total.astype(BF16)
    middle = (total - high.astype(F32)).astype(BF16)
    low = (total - high.astype(F32) - middle.astype(F32)).astype(BF16)
    row = lax.broadcasted_iota(jnp.int32, (16, width), 0)
    packed = jnp.where(row == 0, high.astype(F32), jnp.where(row == 1, middle.astype(F32), low.astype(F32)))
    ends_ref[0:states, :] = state.astype(BF16)
    ends_ref[states : 2 * states, :] = adjoint.astype(BF16)
    ends_ref[2 * states : 2 * states + 16, :] = packed.astype(BF16)


def joined(place_ref, sib_ref, far_ref, rate, s):
    late, upper = place_ref[0] >= 2, place_ref[0] % 2 == 1
    states = rate.shape[0]
    far = far_ref[:, s].astype(F32)
    parts = sib_ref[2 * states : 2 * states + 16, s].astype(F32)
    step = jnp.exp2(rate * (parts[0:1] + parts[1:2] + parts[2:3])) * far
    sib_state, sib_adjoint = sib_ref[0:states, s].astype(F32), sib_ref[states : 2 * states, s].astype(F32)
    state = jnp.where(late, far, 0.0)
    state = jnp.where(upper, sib_state + jnp.where(late, step, 0.0), state)
    adjoint = jnp.where(late, 0.0, far)
    adjoint = jnp.where(upper, adjoint, sib_adjoint + jnp.where(late, 0.0, step))
    return state, adjoint


def main_kernel(direct, place_ref, *refs):
    (x_ref, rim_ref, dy_ref, dls, sig_ref, dus, u_ref, slope_ref, dub_ref, b_ref, c_ref, cw_ref, dl_ref, sk_ref,
     gin_ref, borrow_ref, tail_ref, gb_ref, gc_ref, give_ref, keep_ref,
     xe, dyf, ahs, hb, dpe, rates, naturals, bb_ref, cb2_ref, bd_ref, back) = refs[2:]
    length, width = x_ref.shape
    states = dl_ref.shape[0]
    taps = cw_ref.shape[0]
    blocks = length // BLOCK
    slices = lane_slices(width)
    tiles = range(len(slices))
    skip = sk_ref[...]

    @pl.when(pl.program_id(0) == 0)
    def _():
        gb_ref[...] = jnp.zeros_like(gb_ref)
        gc_ref[...] = jnp.zeros_like(gc_ref)
        widen(b_ref, c_ref, bb_ref, cb2_ref, bd_ref)

    set_rates(dl_ref, rates)
    for j, s in enumerate(slices):
        naturals[j] = (-jnp.exp(dl_ref[:, s])).astype(BF16)
    xe[0:8, :] = jnp.zeros((8, width), F32)
    xe[8 - (taps - 1) : 8, :] = rim_ref[...].astype(F32)
    for b in range(blocks):
        rows = slice(b * BLOCK, (b + 1) * BLOCK)
        xe[8 + b * BLOCK : 8 + (b + 1) * BLOCK, :] = x_ref[rows, :].astype(F32)
        put(dyf, rows, dy_ref[rows, :].astype(F32))
    dpe[0:8, :] = jnp.zeros((8, width), F32)
    dpe[length + 8 : length + 16, :] = jnp.zeros((8, width), F32)
    lane = lax.broadcasted_iota(jnp.int32, (states, length), 1)
    by_rows = (((1,), (1,)), ((), ()))

    def picked(table, product, b):
        for i in range(BLOCK):
            table = jnp.where(lane == b * BLOCK + i, product[i * states : (i + 1) * states], table)
        return table

    if direct:
        state, adjoint = ([ref[:, s] for s in slices] for ref in refs[:2])
    else:
        state, adjoint = zip(*(joined(place_ref, *refs[:2], rates[j], s) for j, s in enumerate(slices)))
        state, adjoint = list(state), list(adjoint)
    for j in tiles:
        back[j] = adjoint[j]
    gc = jnp.zeros((states, length), F32)
    for b in range(blocks):
        for i in range(BLOCK):
            t = b * BLOCK + i
            rows = slice(t * states, (t + 1) * states)
            column = bb_ref[rows, :]
            for j in tiles:
                kept = jnp.exp2(row_of(dls, t, j) * rates[j]) * state[j]
                ahs[j, rows, :] = kept.astype(BF16)
                state[j] = kept + column * row_of(dus, t, j)
                hb[b % 2, j, i * states : (i + 1) * states, :] = state[j].astype(BF16)
        product = lax.dot_general(joined_tiles(hb.at[b % 2]), dy_ref[...], by_rows, preferred_element_type=F32)
        gc = picked(gc, product, b)
    gc_ref[...] += gc

    rows_of = lax.broadcasted_iota(jnp.int32, (BLOCK, BLOCK * states), 0)
    cols_of = lax.broadcasted_iota(jnp.int32, (BLOCK, BLOCK * states), 1)
    over_states = jnp.where(rows_of == cols_of // states, 1.0, 0.0).astype(BF16)
    rows_of = lax.broadcasted_iota(jnp.int32, (states, BLOCK * states), 0)
    cols_of = lax.broadcasted_iota(jnp.int32, (states, BLOCK * states), 1)
    over_steps = jnp.where(rows_of == cols_of % states, 1.0, 0.0).astype(BF16)

    adjoint = [back[j] for j in tiles]
    gb = jnp.zeros((states, length), F32)
    rates_sum = [jnp.zeros((states, 2 * LANES), F32) for _ in range(0, len(slices), 2)]
    sums = [jnp.zeros((8, width), F32) for _ in range(taps + 3)]
    weights = [cw_ref[k : k + 1, :] for k in range(taps)]
    for b in reversed(range(blocks)):
        kept = {}
        for i in reversed(range(BLOCK)):
            t = b * BLOCK + i
            rows = slice(t * states, (t + 1) * states)
            column = cb2_ref[rows, :]
            for j in tiles:
                delta = row_of(dls, t, j)
                g = column * row_of(dyf, t, j) + adjoint[j]
                adjoint[j] = jnp.exp2(delta * rates[j]) * g
                low = g.astype(BF16)
                q = low * ahs[j, rows, :]
                kept[i, j] = low, q * naturals[j], q * delta.astype(BF16)

        def operand(m, which):
            return jnp.concatenate(
                [jnp.concatenate([kept[i, j][which] for i in range(BLOCK)], axis=0) for j in (2 * m, 2 * m + 1)],
                axis=1)

        rows = slice(b * BLOCK, (b + 1) * BLOCK)
        ddu, dwn, product = [], [], None
        for m in range(len(rates_sum)):
            g_block = operand(m, 0)
            ddu.append(jnp.dot(bd_ref[rows, :], g_block, preferred_element_type=F32))
            dwn.append(jnp.dot(over_states, operand(m, 1), preferred_element_type=F32))
            rates_sum[m] = rates_sum[m] + jnp.dot(over_steps, operand(m, 2), preferred_element_type=F32)
            part = lax.dot_general(g_block, dub_ref[:, 2 * m * LANES : 2 * (m + 1) * LANES], by_rows,
                                   preferred_element_type=F32)
            product = part if product is None else product + part
        gb = picked(gb, product, b)
        ddu, dwn = jnp.concatenate(ddu, axis=1), jnp.concatenate(dwn, axis=1)
        dy, u = take(dyf, rows), u_ref[rows, :]
        grad_v = (ddu * u + dwn) * sig_ref[rows, :]
        grad_p = (ddu * take(dls, rows) + skip * dy) * slope_ref[rows, :]
        dpe[8 + b * BLOCK : 8 + (b + 1) * BLOCK, :] = grad_p
        sums[taps] += row_sum(grad_p)
        sums[taps + 1] += row_sum(grad_v)
        sums[taps + 2] += row_sum(dy * u)
        grad_x = weights[taps - 1] * grad_p
        for k in range(taps):
            first = b * BLOCK + 9 - taps + k
            sums[k] += row_sum(grad_p * xe[first : first + BLOCK, :])
            if k < taps - 1:
                first = b * BLOCK + 7 + taps - k
                grad_x = grad_x + weights[k] * dpe[first : first + BLOCK, :]
        gin_ref[rows, :] = grad_x.astype(BF16)
        if b == blocks - 1:
            tail_ref[...] = grad_x
    gb_ref[...] += gb
    rates_sum = jnp.concatenate(rates_sum, axis=1)
    grad_rim = weights[0] * dpe[taps - 1 : taps + 7, :]
    for k in range(1, taps):
        grad_rim = grad_rim + weights[k] * dpe[taps - 1 - k : taps + 7 - k, :]
    borrow_ref[...] = grad_rim[8 - borrow_ref.shape[0] : 8].astype(BF16)
    row = lax.broadcasted_iota(jnp.int32, (8, width), 0)
    packed = jnp.zeros((8, width), F32)
    for k in range(taps + 3):
        packed = jnp.where(row == k, jnp.sum(sums[k], axis=0, keepdims=True), packed)
    step, turns = pl.program_id(0), pl.num_programs(0)

    def give_out(out_ref):
        for j, s in enumerate(slices):
            out_ref[0:states, s] = rates_sum[:, s] * (-jnp.exp(dl_ref[:, s]))
        out_ref[states : states + 8, :] = packed

    @pl.when(step < turns // 2)
    def _():
        give_out(give_ref)

    @pl.when(step >= turns // 2)
    def _():
        give_out(keep_ref)


def flipped(value, axis, bit):
    return lax.ppermute(value, axis, [(k, k ^ bit) for k in range(lax.axis_size(axis))])


def add_up(give, keep):
    inner, outer = lax.axis_size("ctx"), lax.axis_size("dp")
    me = lax.axis_index("ctx")
    if inner & (inner - 1) or outer & (outer - 1) or inner == 1:
        upper = me % 2 == 1
        lower_half, upper_half = jnp.where(upper, give, keep), jnp.where(upper, keep, give)
        return lax.psum(jnp.concatenate([lower_half, upper_half], axis=1), ("dp", "ctx"))
    value = keep + flipped(give, "ctx", 1)
    bits = [1 << k for k in range(1, inner.bit_length() - 1)]
    for bit in bits:
        half = value.shape[1] // 2
        upper = (me // bit) % 2
        give = lax.dynamic_slice_in_dim(value, (1 - upper) * half, half, 1)
        got = flipped(give, "ctx", bit)
        value = lax.dynamic_slice_in_dim(value, upper * half, half, 1) + got
    for k in range(outer.bit_length() - 1):
        value = value + flipped(value, "dp", 1 << k)
    for bit in [*reversed(bits), 1]:
        got = flipped(value, "ctx", bit)
        upper = (me // bit) % 2 == 1
        value = jnp.concatenate([jnp.where(upper, got, value), jnp.where(upper, value, got)], axis=1)
    return value


def entering(ends, decay_log):
    states = decay_log.shape[0]
    count, place = lax.axis_size("ctx"), lax.axis_index("ctx")
    if count == 4:
        late, upper = place >= 2, place % 2 == 1
        sib = flipped(ends, "ctx", 1)
        mine, other = ends.astype(F32), sib.astype(F32)
        passing = jnp.where(late == upper, other, mine)
        onto = jnp.where(late == upper, mine, other)
        if_early = lambda piece: jnp.where(late, piece[states : 2 * states], piece[:states])
        total = passing[2 * states : 2 * states + 1] + passing[2 * states + 1 : 2 * states + 2]
        total = total + passing[2 * states + 2 : 2 * states + 3]
        both = jnp.exp(-jnp.exp(decay_log) * total) * if_early(onto) + if_early(passing)
        return sib, flipped(both.astype(BF16), "ctx", 2)
    rate = -jnp.exp(decay_log)
    gathered = lax.all_gather(ends, "ctx").astype(F32)
    total = gathered[:, 2 * states] + gathered[:, 2 * states + 1] + gathered[:, 2 * states + 2]
    decay = jnp.exp(rate[None] * total[:, None, :])
    state = adjoint = jnp.zeros(decay_log.shape, F32)
    for k in range(count - 1):
        state = jnp.where(k < place, decay[k] * state + gathered[k, :states], state)
    for k in range(count - 1, 0, -1):
        adjoint = jnp.where(k > place, decay[k] * adjoint + gathered[k, states : 2 * states], adjoint)
    return state, adjoint


def whole(a):
    return pl.BlockSpec(a.shape, lambda i, *_: (0,) * a.ndim)


def flat(a):
    return a.reshape(1, a.shape[0])


SHAPE = jax.ShapeDtypeStruct
PARAMS = pltpu.CompilerParams(vmem_limit_bytes=VMEM, dimension_semantics=("arbitrary",))


def call_ends(x, rims, step, dy, b_proj, c_proj, conv_weight, conv_bias, step_bias, decay_log):
    (length, channels), states = x.shape, decay_log.shape[0]
    taps, rim = conv_weight.shape[0], rims.shape[0]
    work = length * states * channels
    tiles = ENDS_WIDTH // LANES
    plain = SHAPE((length, channels), F32)
    long = SHAPE((channels // LANES, length, LANES), F32)
    chunk = lambda rows: pl.BlockSpec((rows, ENDS_WIDTH), lambda i, *_: (0, i))
    tiled = pl.BlockSpec((tiles, length, LANES), lambda i, *_: (i, 0, 0))
    return pl.pallas_call(
        ends_kernel,
        grid=(channels // ENDS_WIDTH,),
        in_specs=[chunk(length), chunk(rim), chunk(length), chunk(length), whole(b_proj), whole(c_proj), chunk(taps),
                  chunk(1), chunk(1), chunk(states)],
        out_specs=[chunk(2 * states + 16), tiled, chunk(length), tiled] + [chunk(length)] * 3,
        scratch_shapes=[pltpu.VMEM((length + 16, ENDS_WIDTH), F32), pltpu.VMEM((tiles, length, LANES), F32),
                        pltpu.VMEM((length * states, LANES), F32),
                        pltpu.VMEM((length // BLOCK, states, BLOCK * states), BF16),
                        pltpu.VMEM((tiles, states, LANES), F32)],
        out_shape=[SHAPE((2 * states + 16, channels), BF16), long, plain, long, plain, plain,
                   SHAPE((length, channels), BF16)],
        compiler_params=PARAMS,
        cost_estimate=pl.CostEstimate(flops=8 * work, bytes_accessed=30 * length * channels, transcendentals=work),
    )(x, rims, step, dy, b_proj, c_proj, conv_weight, flat(conv_bias), flat(step_bias), decay_log)


def call_main(place, entering, x, rims, dy, saved, b_proj, c_proj, conv_weight, decay_log, skip_weight):
    (length, channels), states = x.shape, decay_log.shape[0]
    taps, rim = conv_weight.shape[0], rims.shape[0]
    work = length * states * channels
    tiles = WIDTH // LANES
    turns = channels // WIDTH
    half = turns // 2
    summed = pl.BlockSpec((states, length), lambda i, *_: (0, 0))

    def at(i, place):
        return (i // half + 1 + place[0]) % 2 * half + i % half

    def chunk(rows):
        return pl.BlockSpec((rows, WIDTH), lambda i, place: (0, at(i, place)))

    tiled = pl.BlockSpec((tiles, length, LANES), lambda i, place: (at(i, place), 0, 0))
    give = pl.BlockSpec((states + 8, WIDTH), lambda i, place: (0, jnp.minimum(i, half - 1)))
    keep = pl.BlockSpec((states + 8, WIDTH), lambda i, place: (0, jnp.maximum(i - half, 0)))
    return pl.pallas_call(
        partial(main_kernel, lax.axis_size("ctx") != 4),
        grid_spec=pltpu.PrefetchScalarGridSpec(
            num_scalar_prefetch=1,
            grid=(turns,),
            in_specs=[chunk(a.shape[0]) for a in entering] + [chunk(length), chunk(rim), chunk(length), tiled, chunk(length), tiled] + [chunk(length)] * 3 + [whole(b_proj), whole(c_proj), chunk(taps),
                      chunk(states), chunk(1)],
            out_specs=[chunk(length), chunk(rim), chunk(BLOCK), summed, summed, give, keep],
            scratch_shapes=[pltpu.VMEM((length + 16, WIDTH), F32),
                            pltpu.VMEM((tiles, length, LANES), F32),
                            pltpu.VMEM((tiles, length * states, LANES), BF16),
                            pltpu.VMEM((2, tiles, BLOCK * states, LANES), BF16),
                            pltpu.VMEM((length + 16, WIDTH), F32),
                            pltpu.VMEM((tiles, states, LANES), F32),
                            pltpu.VMEM((tiles, states, LANES), BF16),
                            pltpu.VMEM((length * states, LANES), F32),
                            pltpu.VMEM((length * states, LANES), F32),
                            pltpu.VMEM((length, BLOCK * states), BF16),
                            pltpu.VMEM((tiles, states, LANES), F32)],
        ),
        out_shape=[SHAPE((length, channels), BF16), SHAPE((rim, channels), BF16), SHAPE((BLOCK, channels), F32),
                   SHAPE((states, length), F32), SHAPE((states, length), F32)] + [SHAPE((states + 8, channels // 2), F32)] * 2,
        compiler_params=PARAMS,
        cost_estimate=pl.CostEstimate(flops=20 * work, bytes_accessed=24 * length * channels, transcendentals=2 * work),
    )(place, *entering, x, rims, dy, *saved, b_proj, c_proj, conv_weight, decay_log, flat(skip_weight))


def per_device(scan_input, step_raw, input_proj, output_proj, out_cotangent, conv_weight, conv_bias, step_bias,
               decay_log, skip_weight):
    documents, length, channels = scan_input.shape
    states, taps = decay_log.shape[0], conv_weight.shape[0]
    rim = taps - 1
    count = lax.axis_size("ctx")
    place = lax.axis_index("ctx").astype(jnp.int32).reshape(1)
    forth = [(k, k + 1) for k in range(count - 1)]
    back = [(k + 1, k) for k in range(count - 1)]

    def one(x, step, b_proj, c_proj, dy):
        rims = lax.ppermute(x[length - rim :, :], "ctx", forth)
        ends, *saved = call_ends(x, rims, step, dy, b_proj, c_proj, conv_weight, conv_bias, step_bias, decay_log)
        return call_main(place, entering(ends, decay_log), x, rims, dy, saved, b_proj, c_proj,
                         conv_weight, decay_log, skip_weight)

    outs = []
    for d in range(documents):
        gin, borrow, tail, gb, gc, *sums = one(
            scan_input[d], step_raw[d], input_proj[d], output_proj[d], out_cotangent[d])
        given = lax.ppermute(borrow, "ctx", back).astype(F32)
        tail = (tail + jnp.pad(given, ((BLOCK - rim, 0), (0, 0)))).astype(BF16)
        gin = lax.dynamic_update_slice(gin, tail, (length - BLOCK, 0))
        outs.append((gin, gb, gc, sums))
    sums = add_up(*(sum(parts) for parts in zip(*(o[3] for o in outs))))
    return (
        jnp.stack([o[0] for o in outs]),
        jnp.stack([o[1] for o in outs]),
        jnp.stack([o[2] for o in outs]),
        sums[states : states + taps],
        sums[states + taps],
        sums[states + taps + 1],
        sums[:states],
        sums[states + taps + 2],
    )


def solution(mesh):
    split, columns = P("dp", "ctx", None), P("dp", None, "ctx")
    return jax.shard_map(
        per_device,
        mesh=mesh,
        in_specs=(split, split, columns, columns, split, P(), P(), P(), P(), P()),
        out_specs=(split, columns, columns, P(), P(), P(), P(), P()),
        check_vma=False,
    )
```

```python
import math
from functools import partial

import jax
import jax.numpy as jnp
from jax import lax
from jax.experimental import pallas as pl
from jax.experimental.pallas import tpu as pltpu
from jax.sharding import PartitionSpec as P

F32 = jnp.float32
BF16 = jnp.bfloat16
LOG2E = 1.0 / math.log(2.0)
BLOCK = 16
LANES = 128
WIDTH = 512
ENDS_WIDTH = 1024
VMEM = 60 * 1024 * 1024


def lane_slices(width):
    return [slice(j, j + LANES) for j in range(0, width, LANES)]


def row_of(ref, t, j):
    row = ref[j, pl.ds(t, 8, stride=0), :]
    return jnp.concatenate([row, row], axis=0)


def put(ref, rows, value):
    for j in range(ref.shape[0]):
        ref[j, rows, :] = value[:, j * LANES : (j + 1) * LANES]


def take(ref, rows):
    return jnp.concatenate([ref[j, rows, :] for j in range(ref.shape[0])], axis=1)


def joined_tiles(ref):
    return jnp.concatenate([ref[j] for j in range(ref.shape[0])], axis=1)


def row_sum(value):
    total = value[0:8]
    for r in range(8, value.shape[0], 8):
        total = total + value[r : r + 8]
    return total


def set_rates(dl_ref, rates):
    for j, s in enumerate(lane_slices(dl_ref.shape[1])):
        rates[j] = -jnp.exp(dl_ref[:, s]) * LOG2E


def widen(b_ref, c_ref, bw_ref, cw_ref, bd_ref):
    states, length = b_ref.shape
    for t in range(length):
        rows = slice(t * states, (t + 1) * states)
        bw_ref[rows, :] = jnp.broadcast_to(b_ref[:, t : t + 1], (states, LANES))
        cw_ref[rows, :] = jnp.broadcast_to(c_ref[:, t : t + 1], (states, LANES))
    n = lax.broadcasted_iota(jnp.int32, (states, BLOCK * states), 0)
    m = lax.broadcasted_iota(jnp.int32, (states, BLOCK * states), 1)
    repeat = jnp.where(n == m % states, 1.0, 0.0).astype(BF16)
    spread = lax.dot_general(b_ref[...].astype(BF16), repeat, (((0,), (0,)), ((), ())), preferred_element_type=F32)
    t = lax.broadcasted_iota(jnp.int32, (length, BLOCK * states), 0)
    m = lax.broadcasted_iota(jnp.int32, (length, BLOCK * states), 1)
    bd_ref[...] = jnp.where(t % BLOCK == m // states, spread, 0.0).astype(BF16)


def set_diagonals(proj_ref, diag):
    states, length = proj_ref.shape
    n = lax.broadcasted_iota(jnp.int32, (BLOCK, BLOCK * states), 0)
    m = lax.broadcasted_iota(jnp.int32, (BLOCK, BLOCK * states), 1)
    repeat = jnp.where(n == m // states, 1.0, 0.0).astype(BF16)
    n = lax.broadcasted_iota(jnp.int32, (states, BLOCK * states), 0)
    m = lax.broadcasted_iota(jnp.int32, (states, BLOCK * states), 1)
    for b in range(length // BLOCK):
        columns = proj_ref[:, b * BLOCK : (b + 1) * BLOCK].astype(BF16)
        spread = jnp.dot(columns, repeat, preferred_element_type=F32)
        diag[b] = jnp.where(n == m % states, spread, 0.0).astype(BF16)


def piece_ends(steps, inputs, outputs, b_wide, c_diag, rates, width):
    blocks, states = c_diag.shape[0], c_diag.shape[1]
    tiles = range(width // LANES)
    state = [jnp.zeros((states, LANES), F32) for _ in tiles]
    decay = [jnp.ones((states, LANES), F32) for _ in tiles]
    adjoint = [jnp.zeros((states, 2 * LANES), F32) for _ in tiles[::2]]
    for b in range(blocks):
        terms = [[] for _ in tiles]
        for i in range(BLOCK):
            t = b * BLOCK + i
            column = b_wide[t * states : (t + 1) * states, :]
            for j in tiles:
                a = jnp.exp2(row_of(steps, t, j) * rates[j])
                state[j] = a * state[j] + column * row_of(inputs, t, j)
                decay[j] = decay[j] * a
                terms[j].append((decay[j] * row_of(outputs, t, j)).astype(BF16))
        for m in range(len(adjoint)):
            pair = [jnp.concatenate(terms[j], axis=0) for j in (2 * m, 2 * m + 1)]
            adjoint[m] = adjoint[m] + jnp.dot(c_diag[b], jnp.concatenate(pair, axis=1), preferred_element_type=F32)
    return jnp.concatenate(state, axis=1), jnp.concatenate(adjoint, axis=1)


def ends_kernel(x_ref, rim_ref, step_ref, dy_ref, b_ref, c_ref, cw_ref, cb_ref, sb_ref, dl_ref,
                ends_ref, dls, sig_ref, dus, u_ref, slope_ref, dub_ref,
                xe, dyf, b_wide, c_diag, rates):
    length, width = x_ref.shape
    states, taps = dl_ref.shape[0], cw_ref.shape[0]
    weights = [cw_ref[k : k + 1, :] for k in range(taps)]
    bias, shift = cb_ref[...], sb_ref[...]

    @pl.when(pl.program_id(0) == 0)
    def _():
        for t in range(length):
            b_wide[t * states : (t + 1) * states, :] = jnp.broadcast_to(b_ref[:, t : t + 1], (states, LANES))
        set_diagonals(c_ref, c_diag)

    set_rates(dl_ref, rates)
    total = jnp.zeros((8, width), F32)
    xe[0:8, :] = jnp.zeros((8, width), F32)
    xe[8 - (taps - 1) : 8, :] = rim_ref[...].astype(F32)
    for b in range(length // BLOCK):
        rows = slice(b * BLOCK, (b + 1) * BLOCK)
        xe[8 + b * BLOCK : 8 + (b + 1) * BLOCK, :] = x_ref[rows, :].astype(F32)
        put(dyf, rows, dy_ref[rows, :].astype(F32))
        z = jnp.exp(step_ref[rows, :].astype(F32) + shift)
        series = z * (1.0 - z * (0.5 - z * (1.0 / 3.0 - 0.25 * z)))
        delta = jnp.where(z < 0.015625, series, jnp.log(1.0 + z))
        p = bias
        for k in range(taps):
            first = b * BLOCK + 9 - taps + k
            p = p + weights[k] * xe[first : first + BLOCK, :]
        gate = 1.0 / (1.0 + jnp.exp(-p))
        u = p * gate
        du = delta * u
        put(dls, rows, delta)
        put(dus, rows, du)
        sig_ref[rows, :] = z / (1.0 + z)
        u_ref[rows, :] = u
        slope_ref[rows, :] = gate + u * (1.0 - gate)
        dub_ref[rows, :] = du.astype(BF16)
        total = total + row_sum(delta)
    state, adjoint = piece_ends(dls, dus, dyf, b_wide, c_diag, rates, width)
    total = jnp.sum(total, axis=0, keepdims=True)
    high = total.astype(BF16)
    middle = (total - high.astype(F32)).astype(BF16)
    low = (total - high.astype(F32) - middle.astype(F32)).astype(BF16)
    row = lax.broadcasted_iota(jnp.int32, (16, width), 0)
    packed = jnp.where(row == 0, high.astype(F32), jnp.where(row == 1, middle.astype(F32), low.astype(F32)))
    ends_ref[0:states, :] = state.astype(BF16)
    ends_ref[states : 2 * states, :] = adjoint.astype(BF16)
    ends_ref[2 * states : 2 * states + 16, :] = packed.astype(BF16)


def joined(place_ref, sib_ref, far_ref, rate, s):
    late, upper = place_ref[0] >= 2, place_ref[0] % 2 == 1
    states = rate.shape[0]
    far = far_ref[:, s].astype(F32)
    parts = sib_ref[2 * states : 2 * states + 16, s].astype(F32)
    step = jnp.exp2(rate * (parts[0:1] + parts[1:2] + parts[2:3])) * far
    sib_state, sib_adjoint = sib_ref[0:states, s].astype(F32), sib_ref[states : 2 * states, s].astype(F32)
    state = jnp.where(late, far, 0.0)
    state = jnp.where(upper, sib_state + jnp.where(late, step, 0.0), state)
    adjoint = jnp.where(late, 0.0, far)
    adjoint = jnp.where(upper, adjoint, sib_adjoint + jnp.where(late, 0.0, step))
    return state, adjoint


def main_kernel(direct, place_ref, *refs):
    (x_ref, rim_ref, dy_ref, dls, sig_ref, dus, u_ref, slope_ref, dub_ref, b_ref, c_ref, cw_ref, dl_ref, sk_ref,
     gin_ref, borrow_ref, tail_ref, gb_ref, gc_ref, give_ref, keep_ref,
     xe, dyf, ahs, hb, dpe, rates, naturals, bb_ref, cb2_ref, bd_ref, back) = refs[2:]
    length, width = x_ref.shape
    states = dl_ref.shape[0]
    taps = cw_ref.shape[0]
    blocks = length // BLOCK
    slices = lane_slices(width)
    tiles = range(len(slices))
    skip = sk_ref[...]

    @pl.when(pl.program_id(0) == 0)
    def _():
        gb_ref[...] = jnp.zeros_like(gb_ref)
        gc_ref[...] = jnp.zeros_like(gc_ref)
        widen(b_ref, c_ref, bb_ref, cb2_ref, bd_ref)

    set_rates(dl_ref, rates)
    for j, s in enumerate(slices):
        naturals[j] = (-jnp.exp(dl_ref[:, s])).astype(BF16)
    xe[0:8, :] = jnp.zeros((8, width), F32)
    xe[8 - (taps - 1) : 8, :] = rim_ref[...].astype(F32)
    for b in range(blocks):
        rows = slice(b * BLOCK, (b + 1) * BLOCK)
        xe[8 + b * BLOCK : 8 + (b + 1) * BLOCK, :] = x_ref[rows, :].astype(F32)
        put(dyf, rows, dy_ref[rows, :].astype(F32))
    dpe[0:8, :] = jnp.zeros((8, width), F32)
    dpe[length + 8 : length + 16, :] = jnp.zeros((8, width), F32)
    lane = lax.broadcasted_iota(jnp.int32, (states, length), 1)
    by_rows = (((1,), (1,)), ((), ()))

    def picked(table, product, b):
        for i in range(BLOCK):
            table = jnp.where(lane == b * BLOCK + i, product[i * states : (i + 1) * states], table)
        return table

    if direct:
        state, adjoint = ([ref[:, s] for s in slices] for ref in refs[:2])
    else:
        state, adjoint = zip(*(joined(place_ref, *refs[:2], rates[j], s) for j, s in enumerate(slices)))
        state, adjoint = list(state), list(adjoint)
    for j in tiles:
        back[j] = adjoint[j]
    gc = jnp.zeros((states, length), F32)
    for b in range(blocks):
        for i in range(BLOCK):
            t = b * BLOCK + i
            rows = slice(t * states, (t + 1) * states)
            column = bb_ref[rows, :]
            for j in tiles:
                kept = jnp.exp2(row_of(dls, t, j) * rates[j]) * state[j]
                ahs[j, rows, :] = kept.astype(BF16)
                state[j] = kept + column * row_of(dus, t, j)
                hb[b % 2, j, i * states : (i + 1) * states, :] = state[j].astype(BF16)
        product = lax.dot_general(joined_tiles(hb.at[b % 2]), dy_ref[...], by_rows, preferred_element_type=F32)
        gc = picked(gc, product, b)
    gc_ref[...] += gc

    rows_of = lax.broadcasted_iota(jnp.int32, (BLOCK, BLOCK * states), 0)
    cols_of = lax.broadcasted_iota(jnp.int32, (BLOCK, BLOCK * states), 1)
    over_states = jnp.where(rows_of == cols_of // states, 1.0, 0.0).astype(BF16)
    rows_of = lax.broadcasted_iota(jnp.int32, (states, BLOCK * states), 0)
    cols_of = lax.broadcasted_iota(jnp.int32, (states, BLOCK * states), 1)
    over_steps = jnp.where(rows_of == cols_of % states, 1.0, 0.0).astype(BF16)

    adjoint = [back[j] for j in tiles]
    gb = jnp.zeros((states, length), F32)
    rates_sum = [jnp.zeros((states, 2 * LANES), F32) for _ in range(0, len(slices), 2)]
    sums = [jnp.zeros((8, width), F32) for _ in range(taps + 3)]
    weights = [cw_ref[k : k + 1, :] for k in range(taps)]
    for b in reversed(range(blocks)):
        kept = {}
        for i in reversed(range(BLOCK)):
            t = b * BLOCK + i
            rows = slice(t * states, (t + 1) * states)
            column = cb2_ref[rows, :]
            for j in tiles:
                delta = row_of(dls, t, j)
                g = column * row_of(dyf, t, j) + adjoint[j]
                adjoint[j] = jnp.exp2(delta * rates[j]) * g
                low = g.astype(BF16)
                q = low * ahs[j, rows, :]
                kept[i, j] = low, q * naturals[j], q * delta.astype(BF16)

        def operand(m, which):
            return jnp.concatenate(
                [jnp.concatenate([kept[i, j][which] for i in range(BLOCK)], axis=0) for j in (2 * m, 2 * m + 1)],
                axis=1)

        rows = slice(b * BLOCK, (b + 1) * BLOCK)
        ddu, dwn, product = [], [], None
        for m in range(len(rates_sum)):
            g_block = operand(m, 0)
            ddu.append(jnp.dot(bd_ref[rows, :], g_block, preferred_element_type=F32))
            dwn.append(jnp.dot(over_states, operand(m, 1), preferred_element_type=F32))
            rates_sum[m] = rates_sum[m] + jnp.dot(over_steps, operand(m, 2), preferred_element_type=F32)
            part = lax.dot_general(g_block, dub_ref[:, 2 * m * LANES : 2 * (m + 1) * LANES], by_rows,
                                   preferred_element_type=F32)
            product = part if product is None else product + part
        gb = picked(gb, product, b)
        ddu, dwn = jnp.concatenate(ddu, axis=1), jnp.concatenate(dwn, axis=1)
        dy, u = take(dyf, rows), u_ref[rows, :]
        grad_v = (ddu * u + dwn) * sig_ref[rows, :]
        grad_p = (ddu * take(dls, rows) + skip * dy) * slope_ref[rows, :]
        dpe[8 + b * BLOCK : 8 + (b + 1) * BLOCK, :] = grad_p
        sums[taps] += row_sum(grad_p)
        sums[taps + 1] += row_sum(grad_v)
        sums[taps + 2] += row_sum(dy * u)
        grad_x = weights[taps - 1] * grad_p
        for k in range(taps):
            first = b * BLOCK + 9 - taps + k
            sums[k] += row_sum(grad_p * xe[first : first + BLOCK, :])
            if k < taps - 1:
                first = b * BLOCK + 7 + taps - k
                grad_x = grad_x + weights[k] * dpe[first : first + BLOCK, :]
        gin_ref[rows, :] = grad_x.astype(BF16)
        if b == blocks - 1:
            tail_ref[...] = grad_x
    gb_ref[...] += gb
    rates_sum = jnp.concatenate(rates_sum, axis=1)
    grad_rim = weights[0] * dpe[taps - 1 : taps + 7, :]
    for k in range(1, taps):
        grad_rim = grad_rim + weights[k] * dpe[taps - 1 - k : taps + 7 - k, :]
    borrow_ref[...] = grad_rim[8 - borrow_ref.shape[0] : 8].astype(BF16)
    row = lax.broadcasted_iota(jnp.int32, (8, width), 0)
    packed = jnp.zeros((8, width), F32)
    for k in range(taps + 3):
        packed = jnp.where(row == k, jnp.sum(sums[k], axis=0, keepdims=True), packed)
    step, turns = pl.program_id(0), pl.num_programs(0)

    def give_out(out_ref):
        for j, s in enumerate(slices):
            out_ref[0:states, s] = rates_sum[:, s] * (-jnp.exp(dl_ref[:, s]))
        out_ref[states : states + 8, :] = packed

    @pl.when(step < turns // 2)
    def _():
        give_out(give_ref)

    @pl.when(step >= turns // 2)
    def _():
        give_out(keep_ref)


def flipped(value, axis, bit):
    return lax.ppermute(value, axis, [(k, k ^ bit) for k in range(lax.axis_size(axis))])


def add_up(give, keep):
    inner, outer = lax.axis_size("ctx"), lax.axis_size("dp")
    me = lax.axis_index("ctx")
    if inner & (inner - 1) or outer & (outer - 1) or inner == 1:
        upper = me % 2 == 1
        lower_half, upper_half = jnp.where(upper, give, keep), jnp.where(upper, keep, give)
        return lax.psum(jnp.concatenate([lower_half, upper_half], axis=1), ("dp", "ctx"))
    value = keep + flipped(give, "ctx", 1)
    bits = [1 << k for k in range(1, inner.bit_length() - 1)]
    for bit in bits:
        half = value.shape[1] // 2
        upper = (me // bit) % 2
        give = lax.dynamic_slice_in_dim(value, (1 - upper) * half, half, 1)
        got = flipped(give, "ctx", bit)
        value = lax.dynamic_slice_in_dim(value, upper * half, half, 1) + got
    for k in range(outer.bit_length() - 1):
        value = value + flipped(value, "dp", 1 << k)
    for bit in [*reversed(bits), 1]:
        got = flipped(value, "ctx", bit)
        upper = (me // bit) % 2 == 1
        value = jnp.concatenate([jnp.where(upper, got, value), jnp.where(upper, value, got)], axis=1)
    return value


def entering(ends, decay_log):
    states = decay_log.shape[0]
    count, place = lax.axis_size("ctx"), lax.axis_index("ctx")
    if count == 4:
        late, upper = place >= 2, place % 2 == 1
        sib = flipped(ends, "ctx", 1)
        swap = late == upper
        mine = jnp.where(late, ends[states : 2 * states], ends[:states]).astype(F32)
        other = jnp.where(late, sib[states : 2 * states], sib[:states]).astype(F32)
        parts = [jnp.where(swap, sib[k : k + 1], ends[k : k + 1]).astype(F32) for k in range(2 * states, 2 * states + 3)]
        decay = jnp.exp(-jnp.exp(decay_log) * (parts[0] + parts[1] + parts[2]))
        both = decay * jnp.where(swap, mine, other) + jnp.where(swap, other, mine)
        return sib, flipped(both.astype(BF16), "ctx", 2)
    rate = -jnp.exp(decay_log)
    gathered = lax.all_gather(ends, "ctx").astype(F32)
    total = gathered[:, 2 * states] + gathered[:, 2 * states + 1] + gathered[:, 2 * states + 2]
    decay = jnp.exp(rate[None] * total[:, None, :])
    state = adjoint = jnp.zeros(decay_log.shape, F32)
    for k in range(count - 1):
        state = jnp.where(k < place, decay[k] * state + gathered[k, :states], state)
    for k in range(count - 1, 0, -1):
        adjoint = jnp.where(k > place, decay[k] * adjoint + gathered[k, states : 2 * states], adjoint)
    return state, adjoint


def whole(a):
    return pl.BlockSpec(a.shape, lambda i, *_: (0,) * a.ndim)


def flat(a):
    return a.reshape(1, a.shape[0])


SHAPE = jax.ShapeDtypeStruct
PARAMS = pltpu.CompilerParams(vmem_limit_bytes=VMEM, dimension_semantics=("arbitrary",))


def call_ends(x, rims, step, dy, b_proj, c_proj, conv_weight, conv_bias, step_bias, decay_log):
    (length, channels), states = x.shape, decay_log.shape[0]
    taps, rim = conv_weight.shape[0], rims.shape[0]
    work = length * states * channels
    tiles = ENDS_WIDTH // LANES
    plain = SHAPE((length, channels), F32)
    long = SHAPE((channels // LANES, length, LANES), F32)
    chunk = lambda rows: pl.BlockSpec((rows, ENDS_WIDTH), lambda i, *_: (0, i))
    tiled = pl.BlockSpec((tiles, length, LANES), lambda i, *_: (i, 0, 0))
    return pl.pallas_call(
        ends_kernel,
        grid=(channels // ENDS_WIDTH,),
        in_specs=[chunk(length), chunk(rim), chunk(length), chunk(length), whole(b_proj), whole(c_proj), chunk(taps),
                  chunk(1), chunk(1), chunk(states)],
        out_specs=[chunk(2 * states + 16), tiled, chunk(length), tiled] + [chunk(length)] * 3,
        scratch_shapes=[pltpu.VMEM((length + 16, ENDS_WIDTH), F32), pltpu.VMEM((tiles, length, LANES), F32),
                        pltpu.VMEM((length * states, LANES), F32),
                        pltpu.VMEM((length // BLOCK, states, BLOCK * states), BF16),
                        pltpu.VMEM((tiles, states, LANES), F32)],
        out_shape=[SHAPE((2 * states + 16, channels), BF16), long, plain, long, plain, plain,
                   SHAPE((length, channels), BF16)],
        compiler_params=PARAMS,
        cost_estimate=pl.CostEstimate(flops=8 * work, bytes_accessed=30 * length * channels, transcendentals=work),
    )(x, rims, step, dy, b_proj, c_proj, conv_weight, flat(conv_bias), flat(step_bias), decay_log)


def call_main(place, entering, x, rims, dy, saved, b_proj, c_proj, conv_weight, decay_log, skip_weight):
    (length, channels), states = x.shape, decay_log.shape[0]
    taps, rim = conv_weight.shape[0], rims.shape[0]
    work = length * states * channels
    tiles = WIDTH // LANES
    turns = channels // WIDTH
    half = turns // 2
    summed = pl.BlockSpec((states, length), lambda i, *_: (0, 0))

    def at(i, place):
        return place[1 + i]

    def chunk(rows):
        return pl.BlockSpec((rows, WIDTH), lambda i, place: (0, at(i, place)))

    tiled = pl.BlockSpec((tiles, length, LANES), lambda i, place: (at(i, place), 0, 0))
    give = pl.BlockSpec((states + 8, WIDTH), lambda i, place: (0, jnp.minimum(i, half - 1)))
    keep = pl.BlockSpec((states + 8, WIDTH), lambda i, place: (0, jnp.maximum(i - half, 0)))
    turn = jnp.arange(turns, dtype=jnp.int32)
    place = jnp.concatenate([place, (turn + half * (1 - place % 2)) % turns])
    return pl.pallas_call(
        partial(main_kernel, lax.axis_size("ctx") != 4),
        grid_spec=pltpu.PrefetchScalarGridSpec(
            num_scalar_prefetch=1,
            grid=(turns,),
            in_specs=[chunk(a.shape[0]) for a in entering] + [chunk(length), chunk(rim), chunk(length), tiled, chunk(length), tiled] + [chunk(length)] * 3 + [whole(b_proj), whole(c_proj), chunk(taps),
                      chunk(states), chunk(1)],
            out_specs=[chunk(length), chunk(rim), chunk(BLOCK), summed, summed, give, keep],
            scratch_shapes=[pltpu.VMEM((length + 16, WIDTH), F32),
                            pltpu.VMEM((tiles, length, LANES), F32),
                            pltpu.VMEM((tiles, length * states, LANES), BF16),
                            pltpu.VMEM((2, tiles, BLOCK * states, LANES), BF16),
                            pltpu.VMEM((length + 16, WIDTH), F32),
                            pltpu.VMEM((tiles, states, LANES), F32),
                            pltpu.VMEM((tiles, states, LANES), BF16),
                            pltpu.VMEM((length * states, LANES), F32),
                            pltpu.VMEM((length * states, LANES), F32),
                            pltpu.VMEM((length, BLOCK * states), BF16),
                            pltpu.VMEM((tiles, states, LANES), F32)],
        ),
        out_shape=[SHAPE((length, channels), BF16), SHAPE((rim, channels), BF16), SHAPE((BLOCK, channels), F32),
                   SHAPE((states, length), F32), SHAPE((states, length), F32)] + [SHAPE((states + 8, channels // 2), F32)] * 2,
        compiler_params=PARAMS,
        cost_estimate=pl.CostEstimate(flops=20 * work, bytes_accessed=24 * length * channels, transcendentals=2 * work),
    )(place, *entering, x, rims, dy, *saved, b_proj, c_proj, conv_weight, decay_log, flat(skip_weight))


def per_device(scan_input, step_raw, input_proj, output_proj, out_cotangent, conv_weight, conv_bias, step_bias,
               decay_log, skip_weight):
    documents, length, channels = scan_input.shape
    states, taps = decay_log.shape[0], conv_weight.shape[0]
    rim = taps - 1
    count = lax.axis_size("ctx")
    place = lax.axis_index("ctx").astype(jnp.int32).reshape(1)
    forth = [(k, k + 1) for k in range(count - 1)]
    back = [(k + 1, k) for k in range(count - 1)]

    def one(x, step, b_proj, c_proj, dy):
        rims = lax.ppermute(x[length - rim :, :], "ctx", forth)
        ends, *saved = call_ends(x, rims, step, dy, b_proj, c_proj, conv_weight, conv_bias, step_bias, decay_log)
        return call_main(place, entering(ends, decay_log), x, rims, dy, saved, b_proj, c_proj,
                         conv_weight, decay_log, skip_weight)

    outs = []
    for d in range(documents):
        gin, borrow, tail, gb, gc, *sums = one(
            scan_input[d], step_raw[d], input_proj[d], output_proj[d], out_cotangent[d])
        given = lax.ppermute(borrow, "ctx", back).astype(F32)
        tail = (tail + jnp.pad(given, ((BLOCK - rim, 0), (0, 0)))).astype(BF16)
        gin = lax.dynamic_update_slice(gin, tail, (length - BLOCK, 0))
        outs.append((gin, gb, gc, sums))
    sums = add_up(*(sum(parts) for parts in zip(*(o[3] for o in outs))))
    return (
        jnp.stack([o[0] for o in outs]),
        jnp.stack([o[1] for o in outs]),
        jnp.stack([o[2] for o in outs]),
        sums[states : states + taps],
        sums[states + taps],
        sums[states + taps + 1],
        sums[:states],
        sums[states + taps + 2],
    )


def solution(mesh):
    split, columns = P("dp", "ctx", None), P("dp", None, "ctx")
    return jax.shard_map(
        per_device,
        mesh=mesh,
        in_specs=(split, split, columns, columns, split, P(), P(), P(), P(), P()),
        out_specs=(split, columns, columns, P(), P(), P(), P(), P()),
        check_vma=False,
    )
```
